32 devices in a mesh: dom: 4 (over z), feat: 8 (over y, x, core).
Axes of the slice: x: 2, y: 2, z: 4, core: 2. Of those that a mesh axis runs over, the one named last changes fastest.
Arguments:
- features: bfloat16 [4096, 4096], P('dom', 'feat'), may hold values from -6 to 6
- proj_weight: bfloat16 [3, 4096, 256], P(None, 'feat'), may hold values from -0.75 to 0.75
- source_block: int32 [32, 3, 4], P('dom'), may hold values from 0 to 7
- slot_count: int32 [32, 3], P('dom'), may hold values from 1 to 4
- block_pattern: int32 [32, 3, 4, 8, 128], P('dom'), may hold values from 0 to 65535
- node_type: int32 [4096], P(('dom', 'feat')), may hold values from 0 to 2
- type_gain: float32 [3, 256], replicated, may hold values from 0.1 to 1.9
- cotangent: bfloat16 [4096, 256], P(('dom', 'feat')), may hold values from -6 to 6
Outputs:
- activations: bfloat16 [4096, 256], P(('dom', 'feat'))
- weight_grad: float32 [3, 4096, 256], P(None, 'feat')
The draws below stay inside these ranges and needn't reach their ends.
Inputs may be any that keep to these rules, and one draw needn't show every extreme that they name: `source_block`: a block index within the destination block's own partition. `slot_count`: slots at or past this count are ignored. `block_pattern`: bit j of the word at index w, i marks an edge from source node 16 w + j of the slot's block to node i of the destination block.
All inputs are finite; a program needn't handle non-finite values.
Results may differ from the reference program's by a relative error of at most 0.0055.
Values may be sent and summed in bfloat16 or wider, within the bound.
No kernel may reach another device: no remote copies, remote signals or barrier semaphores. Data moves between devices by JAX's collectives and lax.ppermute only.
A program may use at most 128 MiB of HBM per device.

```python
import jax
import jax.numpy as jnp
from jax import lax

IN_DIM = 4096
HID_DIM = 256
REL = 3
NTYPES = 3
SLOTS = 4
BLK = 128
WORDS = 8
PB = 8
PART_NODES = 1024
NODES = 4096
NBLK = 32
N_DOM = 4


def place_ends(values, own_key, least, top_value):
    dims = values.shape
    index_at = [jax.random.randint(jax.random.fold_in(own_key, axis), (), 0, dims[axis]) for axis in range(len(dims))]
    values = values.at[tuple(index_at)].set(least)
    longest = dims.index(max(dims))
    index_at[longest] = (index_at[longest] + 1) % dims[longest]
    return values.at[tuple(index_at)].set(top_value)


def shard_levels(own_key, shape, split, least, high):
    factor_of, own = 1.0, jax.random.fold_in(own_key, 6)
    for dim, blocks in split:
        draws = jnp.exp(jax.random.uniform(jax.random.fold_in(own, dim), (blocks,), jnp.float32, least / len(split), high / len(split)))
        factor_of = factor_of * jnp.repeat(draws, shape[dim] // blocks).reshape([-1 if axis == dim else 1 for axis in range(len(shape))])
    return factor_of


def scatter_about(own_key, shape, scale, limit, pieces=(), kind=jnp.bfloat16):
    array = scale * jax.random.normal(own_key, shape, jnp.float32)
    if pieces:
        array = array * shard_levels(own_key, shape, pieces, -0.22, 0.18)
    return jnp.clip(array, -limit, limit).astype(kind)


def setup_inputs(seed: int = 0) -> dict:
    arg_keys = jax.random.split(jax.random.key(seed), 9)
    return {
        "features": scatter_about(arg_keys[0], (NODES, IN_DIM), 1.0, 6.0, ((0, 4), (1, 8))),
        "proj_weight": scatter_about(arg_keys[1], (REL, IN_DIM, HID_DIM), (IN_DIM // 64) ** -0.5, 0.75, ((1, 8),)),
        "source_block": place_ends(jax.random.randint(arg_keys[2], (NBLK, REL, SLOTS), 0, PB), jax.random.fold_in(arg_keys[2], 1), 0, PB - 1).astype(jnp.int32),
        "slot_count": place_ends(jax.random.randint(arg_keys[3], (NBLK, REL), 1, SLOTS + 1), jax.random.fold_in(arg_keys[3], 1), 1, SLOTS).astype(jnp.int32),
        "block_pattern": place_ends(jax.random.randint(arg_keys[4], (NBLK, REL, SLOTS, WORDS, BLK), 0, 65536), jax.random.fold_in(arg_keys[4], 1), 0, 65535).astype(jnp.int32),
        "node_type": place_ends(jax.random.randint(arg_keys[5], (NODES,), 0, NTYPES), jax.random.fold_in(arg_keys[5], 1), 0, NTYPES - 1).astype(jnp.int32),
        "type_gain": jnp.clip(1.0 + 0.18 * jax.random.normal(arg_keys[6], (NTYPES, HID_DIM), jnp.float32), 0.1, 1.9),
        "cotangent": scatter_about(arg_keys[7], (NODES, HID_DIM), 1.0, 6.0, ((0, 32),)),
    }


def unpack_bits(packed):
    shifts = (2 ** jnp.arange(16)).astype(jnp.int32)
    bit_values = packed[..., None] // shifts % 2
    bit_values = jnp.swapaxes(bit_values, -3, -2)
    return bit_values.reshape(packed.shape[:-2] + (packed.shape[-1], packed.shape[-2] * 16))

def silu_grad(pre_act):
    sigmoid_value = jax.nn.sigmoid(pre_act)
    return sigmoid_value * (1.0 + pre_act * (1.0 - sigmoid_value))

def type_rows(node_type, type_gain):
    onehot = (node_type[:, None] == jnp.arange(type_gain.shape[0], dtype=jnp.int32)[None, :]).astype(jnp.float32)
    return lax.optimization_barrier(jnp.sum(onehot[:, :, None] * type_gain[None, :, :], axis=1))

def one_partition(partition_item, proj_weight, type_gain):
    features, source_block, slot_count, block_pattern, node_type, cotangent = partition_item
    blocks = features.reshape(PB, BLK, IN_DIM).astype(jnp.float32)
    live_slots = (jnp.arange(SLOTS, dtype=jnp.int32)[None, None, :] < slot_count[:, :, None]).astype(jnp.float32)
    pre_act = jnp.zeros((PART_NODES, HID_DIM), jnp.float32)
    mixed_list = []
    for relation in range(REL):
        summed = jnp.zeros((PB, BLK, IN_DIM), jnp.float32)
        degree = jnp.zeros((PB, BLK), jnp.float32)
        for slot_index in range(SLOTS):
            adjacency = unpack_bits(block_pattern[:, relation, slot_index]).astype(jnp.float32) * live_slots[:, relation, slot_index][:, None, None]
            picked = jnp.take(blocks, source_block[:, relation, slot_index].astype(jnp.int32), axis=0)
            summed = summed + jnp.einsum('bij,bjc->bic', adjacency, picked, precision=lax.Precision.HIGHEST)
            degree = degree + lax.optimization_barrier(jnp.sum(adjacency, axis=2))
        mixed_rows = ((blocks + summed) / (1.0 + degree)[:, :, None]).astype(jnp.bfloat16).reshape(PART_NODES, IN_DIM)
        mixed_list.append(mixed_rows)
        pre_act = pre_act + jnp.dot(mixed_rows, proj_weight[relation], preferred_element_type=jnp.float32)
    row_gains = type_rows(node_type, type_gain)
    output = (jax.nn.silu(pre_act) * row_gains).astype(jnp.bfloat16)
    slope_rows = (cotangent.astype(jnp.float32) * row_gains * silu_grad(pre_act)).astype(jnp.bfloat16)
    weight_grads = jnp.stack([jnp.dot(mixed_one.T, slope_rows, preferred_element_type=jnp.float32) for mixed_one in mixed_list])
    return (output, weight_grads)

def reference(features, proj_weight, source_block, slot_count, block_pattern, node_type, type_gain, cotangent):
    partition_items = (features.reshape(N_DOM, PART_NODES, IN_DIM), source_block.reshape(N_DOM, PB, REL, SLOTS), slot_count.reshape(N_DOM, PB, REL), block_pattern.reshape(N_DOM, PB, REL, SLOTS, WORDS, BLK), node_type.reshape(N_DOM, PART_NODES), cotangent.reshape(N_DOM, PART_NODES, HID_DIM))
    outputs, weight_grads = lax.map(lambda partition_item: one_partition(partition_item, proj_weight, type_gain), partition_items)
    return (outputs.reshape(NODES, HID_DIM), lax.optimization_barrier(jnp.sum(weight_grads, axis=0)))
```

```python
import functools

import jax
import jax.numpy as jnp
from jax import lax
from jax.experimental import pallas as pl
from jax.experimental.pallas import tpu as pltpu
from jax.sharding import PartitionSpec as P

BLK = 128
MIB = 1024 * 1024
BF16 = jnp.bfloat16
F32 = jnp.float32


def unpack_bits(packed):
    shifts = (2 ** jnp.arange(16)).astype(jnp.int32)
    bit_values = packed[..., None] // shifts % 2
    bit_values = jnp.swapaxes(bit_values, -3, -2)
    return bit_values.reshape(packed.shape[:-2] + (packed.shape[-1], packed.shape[-2] * 16))


def silu_grad(pre_act):
    sigmoid_value = jax.nn.sigmoid(pre_act)
    return sigmoid_value * (1.0 + pre_act * (1.0 - sigmoid_value))


def type_rows(node_type, type_gain):
    onehot = (
        node_type[:, None] == jnp.arange(type_gain.shape[0], dtype=jnp.int32)[None, :]
    ).astype(jnp.float32)
    return jnp.sum(onehot[:, :, None] * type_gain[None, :, :], axis=1)


def aggregate(features, source_block, slot_count, block_pattern):
    count_blocks = source_block.shape[0]
    relations = source_block.shape[1]
    slots_each = source_block.shape[2]
    col_width = features.shape[1]
    blocks = features.reshape(count_blocks, BLK, col_width)
    blocks_wide = blocks.astype(jnp.float32)
    live_slots = (
        jnp.arange(slots_each, dtype=jnp.int32)[None, None, :] < slot_count[:, :, None]
    ).astype(jnp.float32)
    mixed_list = []
    for relation in range(relations):
        summed = jnp.zeros((count_blocks, BLK, col_width), jnp.float32)
        degree = jnp.zeros((count_blocks, BLK), jnp.float32)
        for slot_index in range(slots_each):
            adjacency = (
                unpack_bits(block_pattern[:, relation, slot_index]).astype(jnp.float32)
                * live_slots[:, relation, slot_index][:, None, None]
            )
            picked = jnp.take(blocks, source_block[:, relation, slot_index], axis=0)
            summed = summed + jnp.einsum(
                "bij,bjc->bic",
                adjacency.astype(jnp.bfloat16),
                picked,
                preferred_element_type=jnp.float32,
            )
            degree = degree + jnp.sum(adjacency, axis=2)
        mixed_rows = ((blocks_wide + summed) / (1.0 + degree)[:, :, None]).astype(jnp.bfloat16)
        mixed_list.append(mixed_rows.reshape(count_blocks * BLK, col_width))
    return jnp.stack(mixed_list)


def general_body(
    features, proj_weight, source_block, slot_count, block_pattern, node_type, type_gain, cotangent
):
    mixed_all = aggregate(features, source_block, slot_count, block_pattern)
    pre_act = lax.psum_scatter(
        jnp.einsum("rnc,rch->nh", mixed_all, proj_weight, preferred_element_type=jnp.float32),
        "feat",
        scatter_dimension=0,
        tiled=True,
    )
    row_gains = type_rows(node_type, type_gain)
    output = (jax.nn.silu(pre_act) * row_gains).astype(jnp.bfloat16)
    slope_rows = (cotangent.astype(jnp.float32) * row_gains * silu_grad(pre_act)).astype(
        jnp.bfloat16
    )
    local_grad = jnp.einsum(
        "rnc,nh->rch",
        mixed_all,
        lax.all_gather(slope_rows, "feat", axis=0, tiled=True),
        preferred_element_type=jnp.float32,
    )
    weight_grad = lax.psum(local_grad, "dom")
    return (output, weight_grad)


def forward_kernel(
    n_feat, src_ref, cnt_ref, pat_hbm, x_hbm, w_hbm, adj_hbm, deg_ref, *rest
):
    piece_refs = rest[:n_feat]
    pat_ref, x_ref, w_ref, adj_ref, pre_ref, in_sem, out_sem = rest[n_feat:]
    blocks, relations, slots = src_ref.shape
    me = lax.axis_index("feat")

    loads = [
        pltpu.make_async_copy(pat_hbm, pat_ref, in_sem.at[0]),
        pltpu.make_async_copy(x_hbm, x_ref, in_sem.at[1]),
        pltpu.make_async_copy(w_hbm, w_ref, in_sem.at[2]),
    ]
    for load in loads:
        load.start()
    loads[0].wait()

    sub = lax.broadcasted_iota(jnp.int32, (BLK, BLK), 0)
    lane = lax.broadcasted_iota(jnp.int32, (BLK, BLK), 1)
    eye = jnp.where(sub == lane, 1.0, 0.0).astype(BF16)
    bit = jnp.left_shift(1, lax.broadcasted_iota(jnp.int32, (16, BLK), 0))

    def build(relation):
        adj_r = adj_ref.at[relation]
        adj_r[...] = jnp.zeros(adj_r.shape, BF16)
        for b in range(blocks):
            cols = pl.ds(b * BLK, BLK)
            adj_r[b * BLK : (b + 1) * BLK, cols] = eye
            count = cnt_ref[b, relation]
            degree = jnp.zeros((8, BLK), jnp.int32)
            for s in range(slots):
                live = jnp.where(s < count, 0xFFFF, 0)
                words = pat_ref[b, relation, s] & live
                row0 = pl.multiple_of(src_ref[b, relation, s] * BLK, BLK)
                parts = [
                    jnp.where((words[w : w + 1, :] & bit) != 0, 1.0, 0.0)
                    for w in range(words.shape[0])
                ]
                tile = jnp.concatenate(parts, axis=0).astype(BF16)
                adj_r[pl.ds(row0, BLK), cols] += tile
                c = words - ((words >> 1) & 0x5555)
                c = (c & 0x3333) + ((c >> 2) & 0x3333)
                c = (c + (c >> 4)) & 0x0F0F
                degree = degree + ((c + (c >> 8)) & 0x1F)
            total = jnp.sum(degree.astype(F32), axis=0, keepdims=True)
            deg_ref[relation, 0:1, cols] = 1.0 / (1.0 + total)

    stores = []
    for relation in range(relations):
        build(relation)
        store = pltpu.make_async_copy(
            adj_ref.at[relation], adj_hbm.at[relation], out_sem.at[relation]
        )
        store.start()
        stores.append(store)
        if relation == 0:
            loads[1].wait()
            loads[2].wait()
        w_t = w_ref[relation].T
        y_t = lax.dot_general(
            w_t, x_ref[...], (((1,), (1,)), ((), ())), preferred_element_type=F32
        ).astype(BF16)
        p_t = jnp.dot(y_t, adj_ref[relation], preferred_element_type=F32)
        p_t = p_t * deg_ref[relation, 0:1, :]
        if relation == 0:
            pre_ref[...] = p_t
        else:
            pre_ref[...] += p_t

    for k, piece in enumerate(piece_refs):
        first = pl.multiple_of((me ^ k) * BLK, BLK)
        piece[...] = pre_ref[:, pl.ds(first, BLK)].T.astype(BF16)
    for store in stores:
        store.wait()


def forward(features, proj_weight, source_block, slot_count, block_pattern, n_feat):
    nodes, cols = features.shape
    relations, _, hidden = proj_weight.shape
    any_spec = pl.BlockSpec(memory_space=pl.ANY)
    smem = pl.BlockSpec(memory_space=pltpu.SMEM)
    vmem = pl.BlockSpec(memory_space=pltpu.VMEM)
    out = pl.pallas_call(
        functools.partial(forward_kernel, n_feat),
        name="forward",
        out_shape=[
            jax.ShapeDtypeStruct((relations, nodes, nodes), BF16),
            jax.ShapeDtypeStruct((relations, 8, nodes), F32),
        ]
        + [jax.ShapeDtypeStruct((nodes // n_feat, hidden), BF16)] * n_feat,
        in_specs=[smem, smem, any_spec, any_spec, any_spec],
        out_specs=[any_spec, vmem] + [vmem] * n_feat,
        scratch_shapes=[
            pltpu.VMEM(block_pattern.shape, jnp.int32),
            pltpu.VMEM(features.shape, BF16),
            pltpu.VMEM(proj_weight.shape, BF16),
            pltpu.VMEM((relations, nodes, nodes), BF16),
            pltpu.VMEM((hidden, nodes), F32),
            pltpu.SemaphoreType.DMA((3,)),
            pltpu.SemaphoreType.DMA((relations,)),
        ],
        compiler_params=pltpu.CompilerParams(vmem_limit_bytes=40 * MIB),
    )(source_block, slot_count, block_pattern, features, proj_weight)
    return out[0], out[1], list(out[2:])


def prepare_kernel(x_ref, inv_ref, xt_ref, col_ref):
    nodes = x_ref.shape[0]
    for b in range(nodes // BLK):
        rows = slice(b * BLK, (b + 1) * BLK)
        xt_ref[:, rows] = x_ref[rows, :].T
        for r in range(inv_ref.shape[0]):
            wide = jnp.broadcast_to(inv_ref[r, 0:1, rows], (BLK, BLK))
            col_ref[r, rows, :] = wide.T


def prepare(features, inv_deg):
    nodes, cols = features.shape
    relations = inv_deg.shape[0]
    return pl.pallas_call(
        prepare_kernel,
        name="prepare",
        out_shape=[
            jax.ShapeDtypeStruct((cols, nodes), BF16),
            jax.ShapeDtypeStruct((relations, nodes, BLK), F32),
        ],
        compiler_params=pltpu.CompilerParams(vmem_limit_bytes=24 * MIB),
        cost_estimate=pl.CostEstimate(
            flops=2 * nodes * cols, bytes_accessed=6 * nodes * cols, transcendentals=0
        ),
    )(features, inv_deg)


def combine_kernel(n_feat, *refs):
    pieces = refs[:n_feat]
    gain_ref, cot_ref, act_ref, slope_ref = refs[n_feat:]
    pre = pieces[0][...].astype(F32)
    for piece in pieces[1:]:
        pre = pre + piece[...].astype(F32)
    gain = gain_ref[...]
    sig = jax.nn.sigmoid(pre)
    act_ref[...] = (pre * sig * gain).astype(BF16)
    grad = sig * (1.0 + pre * (1.0 - sig))
    slope_ref[...] = (cot_ref[...].astype(F32) * gain * grad).astype(BF16)


def combine(pieces, gain, cotangent):
    shape = jax.ShapeDtypeStruct(cotangent.shape, BF16)
    return pl.pallas_call(
        functools.partial(combine_kernel, len(pieces)),
        name="combine",
        out_shape=[shape, shape],
    )(*pieces, gain, cotangent)


def gradient_kernel(n_feat, relation, xt_ref, adj_ref, col_ref, *rest):
    pieces = rest[:n_feat]
    wide_ref, sent_ref, slope_ref = rest[n_feat:]
    me = lax.axis_index("feat")
    rows = pieces[0].shape[0]
    for k, piece in enumerate(pieces):
        first = pl.multiple_of((me ^ k) * rows, rows)
        inv = col_ref[0, pl.ds(first, rows), :]
        inv = jnp.concatenate([inv] * (piece.shape[1] // BLK), axis=1)
        slope_ref[pl.ds(first, rows), :] = (piece[...].astype(F32) * inv).astype(BF16)
    spread = jnp.dot(adj_ref[0], slope_ref[...], preferred_element_type=F32).astype(BF16)
    grad = jnp.dot(xt_ref[...], spread, preferred_element_type=F32)
    wide_ref[...] = grad
    sent_ref[...] = grad.astype(BF16)


def gradient(relation, x_t, adj, col, pieces):
    cols, nodes = x_t.shape
    hidden = pieces[0].shape[1]
    n_feat = len(pieces)

    def whole(shape):
        return pl.BlockSpec(shape, lambda i: (0,) * len(shape))

    def at_relation(shape):
        return pl.BlockSpec(shape, lambda i: (relation, 0, 0))

    return pl.pallas_call(
        functools.partial(gradient_kernel, n_feat, relation),
        name="gradient",
        grid=(1,),
        out_shape=[
            jax.ShapeDtypeStruct((cols, hidden), F32),
            jax.ShapeDtypeStruct((cols, hidden), BF16),
        ],
        in_specs=[whole(x_t.shape), at_relation((1, nodes, nodes)), at_relation((1, nodes, BLK))]
        + [whole(p.shape) for p in pieces],
        out_specs=[whole((cols, hidden)), whole((cols, hidden))],
        scratch_shapes=[pltpu.VMEM((nodes, hidden), BF16)],
        compiler_params=pltpu.CompilerParams(vmem_limit_bytes=24 * MIB),
        cost_estimate=pl.CostEstimate(
            flops=2 * nodes * hidden * (nodes + cols),
            bytes_accessed=2 * nodes * nodes + 6 * cols * hidden,
            transcendentals=0,
        ),
    )(x_t, adj, col, *pieces)


def rounded(x):
    return lax.reduce_precision(x, 8, 7)


def chain_sum(wide, sent, n_dom):
    half = n_dom // 2
    at = lax.axis_index("dom")
    total = wide
    for hop in range(half - 1):
        perm = [(hop, hop + 1), (n_dom - 1 - hop, n_dom - 2 - hop)]
        total = rounded(total + lax.ppermute(sent, "dom", perm).astype(F32))
        sent = total.astype(BF16)
    got = lax.ppermute(sent, "dom", [(half - 1, half), (half, half - 1)])
    total = rounded(sent.astype(F32) + got.astype(F32))
    sent = total.astype(BF16)
    for hop in range(half - 1):
        low, high = half - 1 - hop, half + hop
        got = lax.ppermute(sent, "dom", [(low, low - 1), (high, high + 1)])
        outside = (at < low) | (at > high)
        sent = jnp.where(outside, got, sent)
    return sent.astype(F32)


def dense_body(
    n_dom,
    n_feat,
    features,
    proj_weight,
    source_block,
    slot_count,
    block_pattern,
    node_type,
    type_gain,
    cotangent,
):
    relations = proj_weight.shape[0]
    adj, inv_deg, pieces = forward(
        features, proj_weight, source_block, slot_count, block_pattern, n_feat
    )

    def exchange(k, value):
        return lax.ppermute(value, "feat", [(i, i ^ k) for i in range(n_feat)])

    received = [pieces[0]] + [exchange(k, pieces[k]) for k in range(1, n_feat)]
    gain = type_rows(node_type, type_gain)
    x_t, col = prepare(features, inv_deg)
    activations, slope = combine(received, gain, cotangent)
    slopes = [slope] + [exchange(k, slope) for k in range(1, n_feat)]
    grads = []
    for relation in range(relations):
        wide, sent = gradient(relation, x_t, adj, col, slopes)
        grads.append(chain_sum(wide, sent, n_dom))
    return activations, jnp.stack(grads)


def body(n_dom, n_feat, *args):
    features, source_block = args[0], args[2]
    nodes = features.shape[0]
    fits = 2 * source_block.shape[1] * nodes * nodes <= 8 * MIB
    pairs_up = n_feat & (n_feat - 1) == 0 and n_dom % 2 == 0
    if fits and pairs_up and nodes == n_feat * BLK:
        return dense_body(n_dom, n_feat, *args)
    return general_body(*args)


def solution(mesh):
    placed = (
        P("dom", "feat"),
        P(None, "feat", None),
        P("dom", None, None),
        P("dom", None),
        P("dom", None, None, None, None),
        P(("dom", "feat")),
        P(),
        P(("dom", "feat"), None),
    )
    return jax.shard_map(
        functools.partial(body, mesh.shape["dom"], mesh.shape["feat"]),
        mesh=mesh,
        in_specs=placed,
        out_specs=(P(("dom", "feat"), None), P(None, "feat", None)),
        check_vma=False,
    )
```

```python
import functools

import jax
import jax.numpy as jnp
from jax import lax
from jax.experimental import pallas as pl
from jax.experimental.pallas import tpu as pltpu
from jax.sharding import PartitionSpec as P

BLK = 128
MIB = 1024 * 1024
BF16 = jnp.bfloat16
F32 = jnp.float32


def unpack_bits(packed):
    shifts = (2 ** jnp.arange(16)).astype(jnp.int32)
    bit_values = packed[..., None] // shifts % 2
    bit_values = jnp.swapaxes(bit_values, -3, -2)
    return bit_values.reshape(packed.shape[:-2] + (packed.shape[-1], packed.shape[-2] * 16))


def silu_grad(pre_act):
    sigmoid_value = jax.nn.sigmoid(pre_act)
    return sigmoid_value * (1.0 + pre_act * (1.0 - sigmoid_value))


def type_rows(node_type, type_gain):
    onehot = (
        node_type[:, None] == jnp.arange(type_gain.shape[0], dtype=jnp.int32)[None, :]
    ).astype(jnp.float32)
    return jnp.sum(onehot[:, :, None] * type_gain[None, :, :], axis=1)


def aggregate(features, source_block, slot_count, block_pattern):
    count_blocks = source_block.shape[0]
    relations = source_block.shape[1]
    slots_each = source_block.shape[2]
    col_width = features.shape[1]
    blocks = features.reshape(count_blocks, BLK, col_width)
    blocks_wide = blocks.astype(jnp.float32)
    live_slots = (
        jnp.arange(slots_each, dtype=jnp.int32)[None, None, :] < slot_count[:, :, None]
    ).astype(jnp.float32)
    mixed_list = []
    for relation in range(relations):
        summed = jnp.zeros((count_blocks, BLK, col_width), jnp.float32)
        degree = jnp.zeros((count_blocks, BLK), jnp.float32)
        for slot_index in range(slots_each):
            adjacency = (
                unpack_bits(block_pattern[:, relation, slot_index]).astype(jnp.float32)
                * live_slots[:, relation, slot_index][:, None, None]
            )
            picked = jnp.take(blocks, source_block[:, relation, slot_index], axis=0)
            summed = summed + jnp.einsum(
                "bij,bjc->bic",
                adjacency.astype(jnp.bfloat16),
                picked,
                preferred_element_type=jnp.float32,
            )
            degree = degree + jnp.sum(adjacency, axis=2)
        mixed_rows = ((blocks_wide + summed) / (1.0 + degree)[:, :, None]).astype(jnp.bfloat16)
        mixed_list.append(mixed_rows.reshape(count_blocks * BLK, col_width))
    return jnp.stack(mixed_list)


def general_body(
    features, proj_weight, source_block, slot_count, block_pattern, node_type, type_gain, cotangent
):
    mixed_all = aggregate(features, source_block, slot_count, block_pattern)
    pre_act = lax.psum_scatter(
        jnp.einsum("rnc,rch->nh", mixed_all, proj_weight, preferred_element_type=jnp.float32),
        "feat",
        scatter_dimension=0,
        tiled=True,
    )
    row_gains = type_rows(node_type, type_gain)
    output = (jax.nn.silu(pre_act) * row_gains).astype(jnp.bfloat16)
    slope_rows = (cotangent.astype(jnp.float32) * row_gains * silu_grad(pre_act)).astype(
        jnp.bfloat16
    )
    local_grad = jnp.einsum(
        "rnc,nh->rch",
        mixed_all,
        lax.all_gather(slope_rows, "feat", axis=0, tiled=True),
        preferred_element_type=jnp.float32,
    )
    weight_grad = lax.psum(local_grad, "dom")
    return (output, weight_grad)


def forward_kernel(
    src_ref, cnt_ref, pat_hbm, x_hbm, w_hbm, inv_ref, out_ref, *rest
):
    relations, slots, blocks = src_ref.shape
    adj_out = rest[:relations]
    pat_ref, x_ref, w_ref, adj_ref, pre_ref, in_sem, out_sem = rest[relations:]

    loads = [
        pltpu.make_async_copy(pat_hbm, pat_ref, in_sem.at[0]),
        pltpu.make_async_copy(x_hbm, x_ref, in_sem.at[1]),
        pltpu.make_async_copy(w_hbm, w_ref, in_sem.at[2]),
    ]
    for load in loads:
        load.start()
    loads[0].wait()

    sub = lax.broadcasted_iota(jnp.int32, (BLK, BLK), 0)
    lane = lax.broadcasted_iota(jnp.int32, (BLK, BLK), 1)
    eye = jnp.where(sub == lane, 1.0, 0.0).astype(BF16)
    bit = jnp.left_shift(1, lax.broadcasted_iota(jnp.int32, (16, BLK), 0))

    def build(relation):
        adj_r = adj_ref.at[relation]
        adj_r[...] = jnp.zeros(adj_r.shape, BF16)
        for b in range(blocks):
            cols = pl.ds(b * BLK, BLK)
            adj_r[b * BLK : (b + 1) * BLK, cols] = eye
            count = cnt_ref[relation, b]
            degree = jnp.zeros((8, BLK), jnp.int32)
            for s in range(slots):
                live = jnp.where(s < count, 0xFFFF, 0)
                words = pat_ref[b, relation, s] & live
                row0 = pl.multiple_of(src_ref[relation, s, b] * BLK, BLK)
                parts = [
                    jnp.where((words[w : w + 1, :] & bit) != 0, 1.0, 0.0)
                    for w in range(words.shape[0])
                ]
                tile = jnp.concatenate(parts, axis=0).astype(BF16)
                adj_r[pl.ds(row0, BLK), cols] += tile
                c = words - ((words >> 1) & 0x5555)
                c = (c & 0x3333) + ((c >> 2) & 0x3333)
                c = (c + (c >> 4)) & 0x0F0F
                degree = degree + ((c + (c >> 8)) & 0x1F)
            total = jnp.sum(degree.astype(F32), axis=0, keepdims=True)
            inv_ref[relation, 0:1, cols] = 1.0 / (1.0 + total)

    stores = []
    for relation in range(relations):
        build(relation)
        store = pltpu.make_async_copy(
            adj_ref.at[relation], adj_out[relation], out_sem.at[relation]
        )
        store.start()
        stores.append(store)
        if relation == 0:
            loads[1].wait()
            loads[2].wait()
        w_t = w_ref[relation].T
        y_t = lax.dot_general(
            w_t, x_ref[...], (((1,), (1,)), ((), ())), preferred_element_type=F32
        ).astype(BF16)
        p_t = jnp.dot(y_t, adj_ref[relation], preferred_element_type=F32)
        p_t = p_t * inv_ref[relation, 0:1, :]
        if relation == 0:
            pre_ref[...] = p_t
        else:
            pre_ref[...] += p_t

    for b in range(blocks):
        rows = slice(b * BLK, (b + 1) * BLK)
        out_ref[rows, :] = pre_ref[:, rows].T.astype(BF16)
    for store in stores:
        store.wait()


def forward(features, proj_weight, source_block, slot_count, block_pattern):
    nodes, cols = features.shape
    relations, _, hidden = proj_weight.shape
    hbm = pl.BlockSpec(memory_space=pltpu.HBM)
    smem = pl.BlockSpec(memory_space=pltpu.SMEM)
    vmem = pl.BlockSpec(memory_space=pltpu.VMEM)
    inv_deg, partial, *adj = pl.pallas_call(
        forward_kernel,
        name="forward",
        out_shape=[
            jax.ShapeDtypeStruct((relations, 8, nodes), F32),
            jax.ShapeDtypeStruct((nodes, hidden), BF16),
        ]
        + [jax.ShapeDtypeStruct((nodes, nodes), BF16)] * relations,
        in_specs=[smem, smem, hbm, hbm, hbm],
        out_specs=[vmem, vmem] + [hbm] * relations,
        scratch_shapes=[
            pltpu.VMEM(block_pattern.shape, jnp.int32),
            pltpu.VMEM(features.shape, BF16),
            pltpu.VMEM(proj_weight.shape, BF16),
            pltpu.VMEM((relations, nodes, nodes), BF16),
            pltpu.VMEM((hidden, nodes), F32),
            pltpu.SemaphoreType.DMA((3,)),
            pltpu.SemaphoreType.DMA((relations,)),
        ],
        compiler_params=pltpu.CompilerParams(vmem_limit_bytes=64 * MIB),
    )(
        jnp.transpose(source_block, (1, 2, 0)),
        jnp.transpose(slot_count, (1, 0)),
        block_pattern,
        features,
        proj_weight,
    )
    return inv_deg, partial, adj


def prepare_kernel(x_ref, inv_ref, xt_ref, *col_refs):
    nodes = x_ref.shape[0]
    for b in range(nodes // BLK):
        rows = slice(b * BLK, (b + 1) * BLK)
        xt_ref[:, rows] = x_ref[rows, :].T
        for r, col_ref in enumerate(col_refs):
            wide = jnp.broadcast_to(inv_ref[r, 0:1, rows], (BLK, BLK))
            col_ref[rows, :] = wide.T


def prepare(features, inv_deg):
    nodes, cols = features.shape
    relations = inv_deg.shape[0]
    x_t, *col = pl.pallas_call(
        prepare_kernel,
        name="prepare",
        out_shape=[jax.ShapeDtypeStruct((cols, nodes), BF16)]
        + [jax.ShapeDtypeStruct((nodes, BLK), F32)] * relations,
        compiler_params=pltpu.CompilerParams(vmem_limit_bytes=12 * MIB),
        cost_estimate=pl.CostEstimate(
            flops=2 * nodes * cols, bytes_accessed=6 * nodes * cols, transcendentals=0
        ),
    )(features, inv_deg)
    return x_t, col


def combine_kernel(n_feat, part_ref, type_ref, gain_ref, cot_ref, act_ref, slope_ref):
    rows = act_ref.shape[0]
    pre = part_ref[0:rows, :].astype(F32)
    for k in range(1, n_feat):
        pre = pre + part_ref[k * rows : (k + 1) * rows, :].astype(F32)
    types = jnp.broadcast_to(type_ref[...].astype(F32), (rows, rows)).T
    types = jnp.concatenate([types] * (act_ref.shape[1] // rows), axis=1)
    gain = jnp.zeros(act_ref.shape, F32)
    for t in range(gain_ref.shape[0]):
        gain = jnp.where(types == t, gain_ref[t : t + 1, :], gain)
    sig = jax.nn.sigmoid(pre)
    act_ref[...] = (pre * sig * gain).astype(BF16)
    grad = sig * (1.0 + pre * (1.0 - sig))
    slope_ref[...] = (cot_ref[...].astype(F32) * gain * grad).astype(BF16)


def combine(partial, node_type, type_gain, cotangent, n_feat):
    shape = jax.ShapeDtypeStruct(cotangent.shape, BF16)
    return pl.pallas_call(
        functools.partial(combine_kernel, n_feat),
        name="combine",
        out_shape=[shape, shape],
        compiler_params=pltpu.CompilerParams(vmem_limit_bytes=6 * MIB),
    )(partial, node_type[None, :], type_gain, cotangent)


def gradient_kernel(
    xt_ref, adj_ref, col_ref, slope_ref, wide_ref, sent_ref, scaled_ref
):
    inv = col_ref[...]
    inv = jnp.concatenate([inv] * (slope_ref.shape[1] // BLK), axis=1)
    scaled_ref[...] = (slope_ref[...].astype(F32) * inv).astype(BF16)
    spread = jnp.dot(adj_ref[...], scaled_ref[...], preferred_element_type=F32).astype(BF16)
    grad = jnp.dot(xt_ref[...], spread, preferred_element_type=F32)
    wide_ref[...] = grad
    sent_ref[...] = grad.astype(BF16)


def gradient(x_t, adj, col, slopes):
    cols, nodes = x_t.shape
    hidden = slopes.shape[1]
    vmem = pl.BlockSpec(memory_space=pltpu.VMEM)
    return pl.pallas_call(
        gradient_kernel,
        name="gradient",
        out_shape=[
            jax.ShapeDtypeStruct((cols, hidden), F32),
            jax.ShapeDtypeStruct((cols, hidden), BF16),
        ],
        in_specs=[vmem] * 4,
        out_specs=[vmem] * 2,
        scratch_shapes=[
            pltpu.VMEM((nodes, hidden), BF16),
        ],
        compiler_params=pltpu.CompilerParams(vmem_limit_bytes=12 * MIB),
        cost_estimate=pl.CostEstimate(
            flops=2 * nodes * hidden * (nodes + cols),
            bytes_accessed=2 * nodes * nodes + 6 * cols * hidden,
            transcendentals=0,
        ),
    )(x_t, adj, col, slopes)


def rounded(x):
    return lax.reduce_precision(x, 8, 7)


def chain_sum(wide, sent, n_dom):
    half = n_dom // 2
    at = lax.axis_index("dom")
    total = wide
    for hop in range(half - 1):
        perm = [(hop, hop + 1), (n_dom - 1 - hop, n_dom - 2 - hop)]
        total = rounded(total + lax.ppermute(sent, "dom", perm).astype(F32))
        sent = total.astype(BF16)
    got = lax.ppermute(sent, "dom", [(half - 1, half), (half, half - 1)])
    total = rounded(sent.astype(F32) + got.astype(F32))
    sent = total.astype(BF16)
    for hop in range(half - 1):
        low, high = half - 1 - hop, half + hop
        got = lax.ppermute(sent, "dom", [(low, low - 1), (high, high + 1)])
        outside = (at < low) | (at > high)
        sent = jnp.where(outside, got, sent)
    return sent.astype(F32)


def dense_body(
    n_dom,
    n_feat,
    features,
    proj_weight,
    source_block,
    slot_count,
    block_pattern,
    node_type,
    type_gain,
    cotangent,
):
    relations = proj_weight.shape[0]
    inv_deg, partial, adj = forward(
        features, proj_weight, source_block, slot_count, block_pattern
    )
    parts = lax.all_to_all(partial, "feat", 0, 0, tiled=True)
    x_t, col = prepare(features, inv_deg)
    activations, slope = combine(parts, node_type, type_gain, cotangent, n_feat)
    slopes = lax.all_gather(slope, "feat", axis=0, tiled=True)
    grads = []
    for relation in range(relations):
        wide, sent = gradient(x_t, adj[relation], col[relation], slopes)
        grads.append(chain_sum(wide, sent, n_dom))
    return activations, jnp.stack(grads)


def body(n_dom, n_feat, *args):
    features, source_block = args[0], args[2]
    nodes = features.shape[0]
    fits = 2 * source_block.shape[1] * nodes * nodes <= 8 * MIB
    pairs_up = n_feat & (n_feat - 1) == 0 and n_dom % 2 == 0
    if fits and pairs_up and nodes == n_feat * BLK:
        return dense_body(n_dom, n_feat, *args)
    return general_body(*args)


def solution(mesh):
    placed = (
        P("dom", "feat"),
        P(None, "feat", None),
        P("dom", None, None),
        P("dom", None),
        P("dom", None, None, None, None),
        P(("dom", "feat")),
        P(),
        P(("dom", "feat"), None),
    )
    return jax.shard_map(
        functools.partial(body, mesh.shape["dom"], mesh.shape["feat"]),
        mesh=mesh,
        in_specs=placed,
        out_specs=(P(("dom", "feat"), None), P(None, "feat", None)),
        check_vma=False,
    )
```

```python
import functools

import jax
import jax.numpy as jnp
from jax import lax
from jax.experimental import pallas as pl
from jax.experimental.pallas import tpu as pltpu
from jax.sharding import PartitionSpec as P

BLK = 128
MIB = 1024 * 1024
BF16 = jnp.bfloat16
F32 = jnp.float32


def unpack_bits(packed):
    shifts = (2 ** jnp.arange(16)).astype(jnp.int32)
    bit_values = packed[..., None] // shifts % 2
    bit_values = jnp.swapaxes(bit_values, -3, -2)
    return bit_values.reshape(packed.shape[:-2] + (packed.shape[-1], packed.shape[-2] * 16))


def silu_grad(pre_act):
    sigmoid_value = jax.nn.sigmoid(pre_act)
    return sigmoid_value * (1.0 + pre_act * (1.0 - sigmoid_value))


def type_rows(node_type, type_gain):
    onehot = (
        node_type[:, None] == jnp.arange(type_gain.shape[0], dtype=jnp.int32)[None, :]
    ).astype(jnp.float32)
    return jnp.sum(onehot[:, :, None] * type_gain[None, :, :], axis=1)


def aggregate(features, source_block, slot_count, block_pattern):
    count_blocks = source_block.shape[0]
    relations = source_block.shape[1]
    slots_each = source_block.shape[2]
    col_width = features.shape[1]
    blocks = features.reshape(count_blocks, BLK, col_width)
    blocks_wide = blocks.astype(jnp.float32)
    live_slots = (
        jnp.arange(slots_each, dtype=jnp.int32)[None, None, :] < slot_count[:, :, None]
    ).astype(jnp.float32)
    mixed_list = []
    for relation in range(relations):
        summed = jnp.zeros((count_blocks, BLK, col_width), jnp.float32)
        degree = jnp.zeros((count_blocks, BLK), jnp.float32)
        for slot_index in range(slots_each):
            adjacency = (
                unpack_bits(block_pattern[:, relation, slot_index]).astype(jnp.float32)
                * live_slots[:, relation, slot_index][:, None, None]
            )
            picked = jnp.take(blocks, source_block[:, relation, slot_index], axis=0)
            summed = summed + jnp.einsum(
                "bij,bjc->bic",
                adjacency.astype(jnp.bfloat16),
                picked,
                preferred_element_type=jnp.float32,
            )
            degree = degree + jnp.sum(adjacency, axis=2)
        mixed_rows = ((blocks_wide + summed) / (1.0 + degree)[:, :, None]).astype(jnp.bfloat16)
        mixed_list.append(mixed_rows.reshape(count_blocks * BLK, col_width))
    return jnp.stack(mixed_list)


def general_body(
    features, proj_weight, source_block, slot_count, block_pattern, node_type, type_gain, cotangent
):
    mixed_all = aggregate(features, source_block, slot_count, block_pattern)
    pre_act = lax.psum_scatter(
        jnp.einsum("rnc,rch->nh", mixed_all, proj_weight, preferred_element_type=jnp.float32),
        "feat",
        scatter_dimension=0,
        tiled=True,
    )
    row_gains = type_rows(node_type, type_gain)
    output = (jax.nn.silu(pre_act) * row_gains).astype(jnp.bfloat16)
    slope_rows = (cotangent.astype(jnp.float32) * row_gains * silu_grad(pre_act)).astype(
        jnp.bfloat16
    )
    local_grad = jnp.einsum(
        "rnc,nh->rch",
        mixed_all,
        lax.all_gather(slope_rows, "feat", axis=0, tiled=True),
        preferred_element_type=jnp.float32,
    )
    weight_grad = lax.psum(local_grad, "dom")
    return (output, weight_grad)


STRIP = 2 * BLK


def halving_offsets(core):
    first = jnp.where(core == 0, 2, 4)
    return first, 6 - first


def forward_kernel(src_ref, cnt_ref, pat_hbm, x_hbm, w_hbm, inv_ref, keep_ref, send_ref, *rest):
    relations, slots, blocks = src_ref.shape
    strips = blocks // 2
    adj_out = rest[:relations]
    rest = rest[relations:]
    adj_refs = [rest[r * strips : (r + 1) * strips] for r in range(relations)]
    pat_ref, x_ref, w_ref, pre_ref, in_sem, out_sem = rest[relations * strips :]

    loads = [
        pltpu.make_async_copy(pat_hbm, pat_ref, in_sem.at[0]),
        pltpu.make_async_copy(x_hbm, x_ref, in_sem.at[1]),
        pltpu.make_async_copy(w_hbm, w_ref, in_sem.at[2]),
    ]
    for load in loads:
        load.start()

    sub = lax.broadcasted_iota(jnp.int32, (BLK, BLK), 0)
    lane = lax.broadcasted_iota(jnp.int32, (BLK, BLK), 1)
    eye = jnp.where(sub == lane, 1.0, 0.0).astype(BF16)
    bit = jnp.left_shift(1, lax.broadcasted_iota(jnp.int32, (16, BLK), 0))

    for strip_refs in adj_refs:
        for i, strip in enumerate(strip_refs):
            strip[...] = jnp.zeros(strip.shape, BF16)
            for b in (2 * i, 2 * i + 1):
                lanes = slice((b % 2) * BLK, (b % 2 + 1) * BLK)
                strip[b * BLK : (b + 1) * BLK, lanes] = eye
    loads[0].wait()

    def build(relation):
        degree = [jnp.zeros((8, BLK), jnp.int32)] * blocks
        for s in range(slots):
            for b in range(blocks):
                strip = adj_refs[relation][b // 2]
                lanes = slice((b % 2) * BLK, (b % 2 + 1) * BLK)
                live = jnp.where(s < cnt_ref[relation, b], 0xFFFF, 0)
                words = pat_ref[b, relation, s] & live
                row0 = pl.multiple_of(src_ref[relation, s, b] * BLK, BLK)
                parts = [
                    jnp.where((words[w : w + 1, :] & bit) != 0, 1.0, 0.0)
                    for w in range(words.shape[0])
                ]
                tile = jnp.concatenate(parts, axis=0).astype(BF16)
                strip[pl.ds(row0, BLK), lanes] += tile
                c = words - ((words >> 1) & 0x5555)
                c = (c & 0x3333) + ((c >> 2) & 0x3333)
                c = (c + (c >> 4)) & 0x0F0F
                degree[b] = degree[b] + ((c + (c >> 8)) & 0x1F)
        for b in range(blocks):
            total = jnp.sum(degree[b].astype(F32), axis=0, keepdims=True)
            inv_ref[relation, 0:1, b * BLK : (b + 1) * BLK] = 1.0 / (1.0 + total)

    stores = []
    for relation in range(relations):
        build(relation)
        for i, strip in enumerate(adj_refs[relation]):
            store = pltpu.make_async_copy(
                strip,
                adj_out[relation].at[:, pl.ds(i * STRIP, STRIP)],
                out_sem.at[relation * strips + i],
            )
            store.start()
            stores.append(store)
        if relation == 0:
            loads[1].wait()
            loads[2].wait()
        w_t = w_ref[relation].T
        y_t = lax.dot_general(
            w_t, x_ref[...], (((1,), (1,)), ((), ())), preferred_element_type=F32
        ).astype(BF16)
        for i, strip in enumerate(adj_refs[relation]):
            lanes = slice(i * STRIP, (i + 1) * STRIP)
            p_t = jnp.dot(y_t, strip[...], preferred_element_type=F32)
            p_t = p_t * inv_ref[relation, 0:1, lanes]
            if relation == 0:
                pre_ref[:, lanes] = p_t
            else:
                pre_ref[:, lanes] += p_t

    me = lax.axis_index("feat")
    one, two = halving_offsets(me % 2)

    def block(k):
        return pre_ref[:, pl.ds(pl.multiple_of((me ^ k) * BLK, BLK), BLK)].T

    for i, k in enumerate((1, 1 ^ one, 1 ^ two, 7)):
        send_ref[i * BLK : (i + 1) * BLK, :] = block(k).astype(BF16)
    for i, k in enumerate((0, two, one, 6)):
        keep_ref[i * BLK : (i + 1) * BLK, :] = block(k)
    for store in stores:
        store.wait()


def forward(features, proj_weight, source_block, slot_count, block_pattern):
    nodes, cols = features.shape
    relations, _, hidden = proj_weight.shape
    strips = nodes // STRIP
    hbm = pl.BlockSpec(memory_space=pltpu.HBM)
    smem = pl.BlockSpec(memory_space=pltpu.SMEM)
    vmem = pl.BlockSpec(memory_space=pltpu.VMEM)
    inv_deg, keep, send, *adj = pl.pallas_call(
        forward_kernel,
        name="forward",
        out_shape=[
            jax.ShapeDtypeStruct((relations, 8, nodes), F32),
            jax.ShapeDtypeStruct((nodes // 2, hidden), F32),
            jax.ShapeDtypeStruct((nodes // 2, hidden), BF16),
        ]
        + [jax.ShapeDtypeStruct((nodes, nodes), BF16)] * relations,
        in_specs=[smem, smem, hbm, hbm, hbm],
        out_specs=[vmem] * 3 + [hbm] * relations,
        scratch_shapes=[pltpu.VMEM((nodes, STRIP), BF16)] * (relations * strips)
        + [
            pltpu.VMEM(block_pattern.shape, jnp.int32),
            pltpu.VMEM(features.shape, BF16),
            pltpu.VMEM(proj_weight.shape, BF16),
            pltpu.VMEM((hidden, nodes), F32),
            pltpu.SemaphoreType.DMA((3,)),
            pltpu.SemaphoreType.DMA((relations * strips,)),
        ],
        compiler_params=pltpu.CompilerParams(vmem_limit_bytes=64 * MIB),
    )(
        jnp.transpose(source_block, (1, 2, 0)),
        jnp.transpose(slot_count, (1, 0)),
        block_pattern,
        features,
        proj_weight,
    )
    return inv_deg, keep, send, adj


def halve(keep, send):
    def swap(value, step):
        def partner(f):
            order = (2, 4) if f % 2 == 0 else (4, 2)
            return f ^ (1, order[0], order[1])[step]

        return lax.ppermute(value, "feat", [(f, partner(f)) for f in range(8)])

    got1 = swap(send, 0)
    half, rows = keep.shape[0] // 2, keep.shape[0] // 4
    sent2 = (keep[half:] + got1[half:].astype(F32)).astype(BF16)
    got2 = swap(sent2, 1)
    sent3 = keep[rows:half] + got1[rows:half].astype(F32) + got2[rows:].astype(F32)
    got3 = swap(sent3.astype(BF16), 2)
    return keep, got1, got2, got3


def combine_kernel(
    keep_ref, got1_ref, got2_ref, got3_ref, type_ref, gain_ref, cot_ref, act_ref, slope_ref
):
    rows = act_ref.shape[0]
    pre = keep_ref[...] + got1_ref[...].astype(F32)
    pre = pre + got2_ref[...].astype(F32) + got3_ref[...].astype(F32)
    types = jnp.broadcast_to(type_ref[...].astype(F32), (rows, rows)).T
    types = jnp.concatenate([types] * (act_ref.shape[1] // rows), axis=1)
    gain = jnp.zeros(act_ref.shape, F32)
    for t in range(gain_ref.shape[0]):
        gain = jnp.where(types == t, gain_ref[t : t + 1, :], gain)
    sig = jax.nn.sigmoid(pre)
    act_ref[...] = (pre * sig * gain).astype(BF16)
    grad = sig * (1.0 + pre * (1.0 - sig))
    slope_ref[...] = (cot_ref[...].astype(F32) * gain * grad).astype(BF16)


def combine(parts, node_type, type_gain, cotangent):
    shape = cotangent.shape
    first = pl.BlockSpec(shape, lambda i: (0, 0))
    return pl.pallas_call(
        combine_kernel,
        name="combine",
        grid=(1,),
        out_shape=[jax.ShapeDtypeStruct(shape, BF16)] * 2,
        in_specs=[first] * 4
        + [
            pl.BlockSpec((1, shape[0]), lambda i: (0, 0)),
            pl.BlockSpec(type_gain.shape, lambda i: (0, 0)),
            first,
        ],
        out_specs=[first] * 2,
        compiler_params=pltpu.CompilerParams(vmem_limit_bytes=6 * MIB),
    )(*parts, node_type[None, :], type_gain, cotangent)


def gradient_kernel(
    relation, x_hbm, adj_hbm, inv_hbm, slope_hbm, wide_ref, sent_ref,
    x_ref, adj_ref, inv_ref, slope_ref, scaled_ref, sem,
):
    nodes = x_ref.shape[0]
    step = nodes // 4
    loads = [
        pltpu.make_async_copy(inv_hbm.at[relation], inv_ref, sem.at[0]),
        pltpu.make_async_copy(slope_hbm, slope_ref, sem.at[1]),
    ]
    for i in range(4):
        rows = pl.ds(i * step, step)
        loads.append(pltpu.make_async_copy(adj_hbm.at[rows], adj_ref.at[rows], sem.at[2 + 2 * i]))
        loads.append(pltpu.make_async_copy(x_hbm.at[rows], x_ref.at[rows], sem.at[3 + 2 * i]))
    for load in loads:
        load.start()
    loads[0].wait()
    loads[1].wait()
    for b in range(nodes // BLK):
        rows = slice(b * BLK, (b + 1) * BLK)
        inv = jnp.broadcast_to(inv_ref[0:1, rows], (BLK, BLK)).T
        inv = jnp.concatenate([inv] * (slope_ref.shape[1] // BLK), axis=1)
        scaled_ref[rows, :] = (slope_ref[rows, :].astype(F32) * inv).astype(BF16)
    grad = None
    for i in range(4):
        rows = slice(i * step, (i + 1) * step)
        loads[2 + 2 * i].wait()
        loads[3 + 2 * i].wait()
        spread = jnp.dot(adj_ref[rows, :], scaled_ref[...], preferred_element_type=F32)
        part = jnp.dot(x_ref[rows, :].T, spread.astype(BF16), preferred_element_type=F32)
        grad = part if grad is None else grad + part
    wide_ref[...] = grad
    sent_ref[...] = grad.astype(BF16)


def gradient(relation, features, adj, inv_deg, slopes):
    nodes, cols = features.shape
    hidden = slopes.shape[1]
    hbm = pl.BlockSpec(memory_space=pltpu.HBM)
    vmem = pl.BlockSpec(memory_space=pltpu.VMEM)
    return pl.pallas_call(
        functools.partial(gradient_kernel, relation),
        name="gradient",
        out_shape=[
            jax.ShapeDtypeStruct((cols, hidden), F32),
            jax.ShapeDtypeStruct((cols, hidden), BF16),
        ],
        in_specs=[hbm] * 4,
        out_specs=[vmem] * 2,
        scratch_shapes=[
            pltpu.VMEM((nodes, cols), BF16),
            pltpu.VMEM((nodes, nodes), BF16),
            pltpu.VMEM((8, nodes), F32),
            pltpu.VMEM((nodes, hidden), BF16),
            pltpu.VMEM((nodes, hidden), BF16),
            pltpu.SemaphoreType.DMA((10,)),
        ],
        compiler_params=pltpu.CompilerParams(vmem_limit_bytes=64 * MIB),
        cost_estimate=pl.CostEstimate(
            flops=2 * nodes * hidden * (nodes + cols),
            bytes_accessed=2 * nodes * nodes + 6 * cols * hidden,
            transcendentals=0,
        ),
    )(features, adj, inv_deg, slopes)


def rounded(x):
    return lax.reduce_precision(x, 8, 7)


def chain_sum(chunks, n_dom):
    half = n_dom // 2
    at = lax.axis_index("dom")
    inner = []
    for wide, sent in chunks:
        for hop in range(half - 1):
            perm = [(hop, hop + 1), (n_dom - 1 - hop, n_dom - 2 - hop)]
            wide = rounded(wide + lax.ppermute(sent, "dom", perm).astype(F32))
            sent = wide.astype(BF16)
        inner.append(sent)
    middle = []
    for i, sent in enumerate(inner):
        if i >= 2:
            sent, _ = lax.optimization_barrier((sent, middle[i - 2]))
        got = lax.ppermute(sent, "dom", [(half - 1, half), (half, half - 1)])
        middle.append(rounded(sent.astype(F32) + got.astype(F32)).astype(BF16))
    outer = []
    for i, sent in enumerate(middle):
        if i >= 2:
            sent, outer[i - 2] = lax.optimization_barrier((sent, outer[i - 2]))
        for hop in range(half - 1):
            low, high = half - 1 - hop, half + hop
            got = lax.ppermute(sent, "dom", [(low, low - 1), (high, high + 1)])
            sent = jnp.where((at < low) | (at > high), got, sent)
        outer.append(sent)
    return [sent.astype(F32) for sent in outer]


def dense_body(
    n_dom,
    features,
    proj_weight,
    source_block,
    slot_count,
    block_pattern,
    node_type,
    type_gain,
    cotangent,
):
    inv_deg, keep, send, adj = forward(
        features, proj_weight, source_block, slot_count, block_pattern
    )
    parts = halve(keep, send)
    activations, slope = combine(parts, node_type, type_gain, cotangent)
    slopes = lax.all_gather(slope, "feat", axis=0, tiled=True)
    chunks = [
        gradient(relation, features, adj[relation], inv_deg, slopes)
        for relation in range(proj_weight.shape[0])
    ]
    return activations, jnp.stack(chain_sum(chunks, n_dom))


def body(n_dom, n_feat, *args):
    nodes, relations = args[0].shape[0], args[2].shape[1]
    fits = 2 * relations * nodes * nodes <= 8 * MIB
    if fits and n_feat == 8 and n_dom % 2 == 0 and nodes == n_feat * BLK:
        return dense_body(n_dom, *args)
    return general_body(*args)


def solution(mesh):
    placed = (
        P("dom", "feat"),
        P(None, "feat", None),
        P("dom", None, None),
        P("dom", None),
        P("dom", None, None, None, None),
        P(("dom", "feat")),
        P(),
        P(("dom", "feat"), None),
    )
    return jax.shard_map(
        functools.partial(body, mesh.shape["dom"], mesh.shape["feat"]),
        mesh=mesh,
        in_specs=placed,
        out_specs=(P(("dom", "feat"), None), P(None, "feat", None)),
        check_vma=False,
    )
```

```python
import functools

import jax
import jax.numpy as jnp
from jax import lax
from jax.experimental import pallas as pl
from jax.experimental.pallas import tpu as pltpu
from jax.sharding import PartitionSpec as P

BLK = 128
MIB = 1024 * 1024
BF16 = jnp.bfloat16
F32 = jnp.float32


def unpack_bits(packed):
    shifts = (2 ** jnp.arange(16)).astype(jnp.int32)
    bit_values = packed[..., None] // shifts % 2
    bit_values = jnp.swapaxes(bit_values, -3, -2)
    return bit_values.reshape(packed.shape[:-2] + (packed.shape[-1], packed.shape[-2] * 16))


def silu_grad(pre_act):
    sigmoid_value = jax.nn.sigmoid(pre_act)
    return sigmoid_value * (1.0 + pre_act * (1.0 - sigmoid_value))


def type_rows(node_type, type_gain):
    onehot = (
        node_type[:, None] == jnp.arange(type_gain.shape[0], dtype=jnp.int32)[None, :]
    ).astype(jnp.float32)
    return jnp.sum(onehot[:, :, None] * type_gain[None, :, :], axis=1)


def aggregate(features, source_block, slot_count, block_pattern):
    count_blocks = source_block.shape[0]
    relations = source_block.shape[1]
    slots_each = source_block.shape[2]
    col_width = features.shape[1]
    blocks = features.reshape(count_blocks, BLK, col_width)
    blocks_wide = blocks.astype(jnp.float32)
    live_slots = (
        jnp.arange(slots_each, dtype=jnp.int32)[None, None, :] < slot_count[:, :, None]
    ).astype(jnp.float32)
    mixed_list = []
    for relation in range(relations):
        summed = jnp.zeros((count_blocks, BLK, col_width), jnp.float32)
        degree = jnp.zeros((count_blocks, BLK), jnp.float32)
        for slot_index in range(slots_each):
            adjacency = (
                unpack_bits(block_pattern[:, relation, slot_index]).astype(jnp.float32)
                * live_slots[:, relation, slot_index][:, None, None]
            )
            picked = jnp.take(blocks, source_block[:, relation, slot_index], axis=0)
            summed = summed + jnp.einsum(
                "bij,bjc->bic",
                adjacency.astype(jnp.bfloat16),
                picked,
                preferred_element_type=jnp.float32,
            )
            degree = degree + jnp.sum(adjacency, axis=2)
        mixed_rows = ((blocks_wide + summed) / (1.0 + degree)[:, :, None]).astype(jnp.bfloat16)
        mixed_list.append(mixed_rows.reshape(count_blocks * BLK, col_width))
    return jnp.stack(mixed_list)


def general_body(
    features, proj_weight, source_block, slot_count, block_pattern, node_type, type_gain, cotangent
):
    mixed_all = aggregate(features, source_block, slot_count, block_pattern)
    pre_act = lax.psum_scatter(
        jnp.einsum("rnc,rch->nh", mixed_all, proj_weight, preferred_element_type=jnp.float32),
        "feat",
        scatter_dimension=0,
        tiled=True,
    )
    row_gains = type_rows(node_type, type_gain)
    output = (jax.nn.silu(pre_act) * row_gains).astype(jnp.bfloat16)
    slope_rows = (cotangent.astype(jnp.float32) * row_gains * silu_grad(pre_act)).astype(
        jnp.bfloat16
    )
    local_grad = jnp.einsum(
        "rnc,nh->rch",
        mixed_all,
        lax.all_gather(slope_rows, "feat", axis=0, tiled=True),
        preferred_element_type=jnp.float32,
    )
    weight_grad = lax.psum(local_grad, "dom")
    return (output, weight_grad)


def live_words(relation, slot, b, cnt_ref, pat_ref):
    live = jnp.where(slot < cnt_ref[relation, b], 0xFFFF, 0)
    return pat_ref[b, relation, slot] & live


def start_adjacency(places):
    sub = lax.broadcasted_iota(jnp.int32, (BLK, BLK), 0)
    lane = lax.broadcasted_iota(jnp.int32, (BLK, BLK), 1)
    eye = jnp.where(sub == lane, 1.0, 0.0).astype(BF16)
    for b, (ref, lanes) in enumerate(places):
        ref[:, lanes] = jnp.zeros((ref.shape[0], BLK), BF16)
        ref[b * BLK : (b + 1) * BLK, lanes] = eye


def add_edges(relation, places, src_ref, cnt_ref, pat_ref):
    bit = jnp.left_shift(1, lax.broadcasted_iota(jnp.int32, (16, BLK), 0))
    for s in range(src_ref.shape[1]):
        for b, (ref, lanes) in enumerate(places):
            words = live_words(relation, s, b, cnt_ref, pat_ref)
            row0 = pl.multiple_of(src_ref[relation, s, b] * BLK, BLK)
            parts = [
                jnp.where((words[w : w + 1, :] & bit) != 0, 1.0, 0.0)
                for w in range(words.shape[0])
            ]
            ref[pl.ds(row0, BLK), lanes] += jnp.concatenate(parts, axis=0).astype(BF16)


def inverse_degrees(relation, inv_ref, src_ref, cnt_ref, pat_ref):
    for b in range(src_ref.shape[2]):
        degree = jnp.zeros((8, BLK), jnp.int32)
        for s in range(src_ref.shape[1]):
            words = live_words(relation, s, b, cnt_ref, pat_ref)
            c = words - ((words >> 1) & 0x5555)
            c = (c & 0x3333) + ((c >> 2) & 0x3333)
            c = (c + (c >> 4)) & 0x0F0F
            degree = degree + ((c + (c >> 8)) & 0x1F)
        total = jnp.sum(degree.astype(F32), axis=0, keepdims=True)
        inv_ref[relation, 0:1, b * BLK : (b + 1) * BLK] = 1.0 / (1.0 + total)


def forward_kernel(n_feat, src_ref, cnt_ref, pat_ref, x_ref, w_ref, inv_ref, *rest):
    relations, slots, blocks = src_ref.shape
    piece_refs, adj_refs = rest[:n_feat], rest[n_feat : n_feat + relations]
    pre_ref = rest[n_feat + relations]
    places = [
        [(adj_ref, slice(b * BLK, (b + 1) * BLK)) for b in range(blocks)] for adj_ref in adj_refs
    ]

    for relation in range(relations):
        start_adjacency(places[relation])
    for relation in range(relations):
        inverse_degrees(relation, inv_ref, src_ref, cnt_ref, pat_ref)
        add_edges(relation, places[relation], src_ref, cnt_ref, pat_ref)
        y_t = lax.dot_general(
            w_ref[relation].T, x_ref[...], (((1,), (1,)), ((), ())), preferred_element_type=F32
        ).astype(BF16)
        p_t = jnp.dot(y_t, adj_refs[relation][...], preferred_element_type=F32)
        p_t = p_t * inv_ref[relation, 0:1, :]
        if relation == 0:
            pre_ref[...] = p_t
        else:
            pre_ref[...] += p_t

    me = lax.axis_index("feat")
    for k, piece in enumerate(piece_refs):
        first = pl.multiple_of((me ^ k) * BLK, BLK)
        piece[...] = pre_ref[:, pl.ds(first, BLK)].T.astype(BF16)


def forward(features, proj_weight, source_block, slot_count, block_pattern, n_feat):
    nodes, cols = features.shape
    relations, _, hidden = proj_weight.shape
    smem = pl.BlockSpec(memory_space=pltpu.SMEM)
    vmem = pl.BlockSpec(memory_space=pltpu.VMEM)
    inv_deg, *out = pl.pallas_call(
        functools.partial(forward_kernel, n_feat),
        name="forward",
        out_shape=[jax.ShapeDtypeStruct((relations, 8, nodes), F32)]
        + [jax.ShapeDtypeStruct((nodes // n_feat, hidden), BF16)] * n_feat
        + [jax.ShapeDtypeStruct((nodes, nodes), BF16)] * relations,
        in_specs=[smem, smem, vmem, vmem, vmem],
        out_specs=[vmem] * (1 + n_feat + relations),
        scratch_shapes=[pltpu.VMEM((hidden, nodes), F32)],
        compiler_params=pltpu.CompilerParams(vmem_limit_bytes=24 * MIB),
    )(source_block, slot_count, block_pattern, features, proj_weight)
    return inv_deg, out[:n_feat], out[n_feat:]


def transposed_kernel(x_ref, inv_ref, xt_ref, *col_refs):
    nodes = x_ref.shape[0]
    for b in range(nodes // BLK):
        rows = slice(b * BLK, (b + 1) * BLK)
        xt_ref[:, rows] = x_ref[rows, :].T
        for r, col_ref in enumerate(col_refs):
            wide = jnp.broadcast_to(inv_ref[r, 0:1, rows], (BLK, BLK))
            col_ref[rows, :] = wide.T


def transposed(features, inv_deg):
    nodes, cols = features.shape
    relations = inv_deg.shape[0]
    x_t, *col = pl.pallas_call(
        transposed_kernel,
        name="transposed",
        out_shape=[jax.ShapeDtypeStruct((cols, nodes), BF16)]
        + [jax.ShapeDtypeStruct((nodes, BLK), F32)] * relations,
        compiler_params=pltpu.CompilerParams(vmem_limit_bytes=8 * MIB),
        cost_estimate=pl.CostEstimate(
            flops=2 * nodes * cols, bytes_accessed=6 * nodes * cols, transcendentals=0
        ),
    )(features, inv_deg)
    return x_t, col


def combine_kernel(n_feat, *refs):
    type_ref, gain_ref, cot_ref, act_ref, slope_ref = refs[n_feat:]
    rows = act_ref.shape[0]
    pre = refs[0][...].astype(F32)
    for piece in refs[1:n_feat]:
        pre = pre + piece[...].astype(F32)
    types = jnp.broadcast_to(type_ref[...].astype(F32), (rows, rows)).T
    types = jnp.concatenate([types] * (act_ref.shape[1] // rows), axis=1)
    gain = jnp.zeros(act_ref.shape, F32)
    for t in range(gain_ref.shape[0]):
        gain = jnp.where(types == t, gain_ref[t : t + 1, :], gain)
    sig = jax.nn.sigmoid(pre)
    act_ref[...] = (pre * sig * gain).astype(BF16)
    grad = sig * (1.0 + pre * (1.0 - sig))
    slope_ref[...] = (cot_ref[...].astype(F32) * gain * grad).astype(BF16)


def combine(pieces, node_type, type_gain, cotangent):
    return pl.pallas_call(
        functools.partial(combine_kernel, len(pieces)),
        name="combine",
        out_shape=[jax.ShapeDtypeStruct(cotangent.shape, BF16)] * 2,
        compiler_params=pltpu.CompilerParams(vmem_limit_bytes=6 * MIB),
    )(*pieces, node_type[None, :], type_gain, cotangent)


def gradient_kernel(n_feat, xt_ref, adj_ref, col_ref, *rest):
    sent_ref, scaled_ref = rest[n_feat:]
    me = lax.axis_index("feat")
    for k, piece in zip(ORDER, rest[:n_feat]):
        rows = pl.ds(pl.multiple_of((me ^ k) * BLK, BLK), BLK)
        inv = jnp.concatenate([col_ref[rows, :]] * (piece.shape[1] // BLK), axis=1)
        scaled_ref[rows, :] = (piece[...].astype(F32) * inv).astype(BF16)
    spread = jnp.dot(adj_ref[...], scaled_ref[...], preferred_element_type=F32).astype(BF16)
    grad = jnp.dot(xt_ref[...], spread, preferred_element_type=F32)
    sent_ref[...] = grad.astype(BF16)


def gradient(x_t, adj, col, slopes):
    cols, nodes = x_t.shape
    hidden = slopes[0].shape[1]
    vmem = pl.BlockSpec(memory_space=pltpu.VMEM)
    return pl.pallas_call(
        functools.partial(gradient_kernel, len(slopes)),
        name="gradient",
        out_shape=jax.ShapeDtypeStruct((cols, hidden), BF16),
        in_specs=[vmem] * (3 + len(slopes)),
        out_specs=vmem,
        scratch_shapes=[pltpu.VMEM((nodes, hidden), BF16)],
        compiler_params=pltpu.CompilerParams(vmem_limit_bytes=8 * MIB),
        cost_estimate=pl.CostEstimate(
            flops=2 * nodes * hidden * (nodes + cols),
            bytes_accessed=2 * nodes * nodes + 6 * cols * hidden,
            transcendentals=0,
        ),
    )(x_t, adj, col, *slopes)


def rounded(x):
    return lax.reduce_precision(x, 8, 7)


def chain_sum(chunks, n_dom):
    half = n_dom // 2
    at = lax.axis_index("dom")
    inner = []
    for sent in chunks:
        for hop in range(half - 1):
            perm = [(hop, hop + 1), (n_dom - 1 - hop, n_dom - 2 - hop)]
            got = lax.ppermute(sent, "dom", perm)
            sent = rounded(sent.astype(F32) + got.astype(F32)).astype(BF16)
        inner.append(sent)
    middle = []
    for i, sent in enumerate(inner):
        if i >= 2:
            sent, _ = lax.optimization_barrier((sent, middle[i - 2]))
        got = lax.ppermute(sent, "dom", [(half - 1, half), (half, half - 1)])
        middle.append(rounded(sent.astype(F32) + got.astype(F32)).astype(BF16))
    outer = []
    for i, sent in enumerate(middle):
        if i >= 2:
            sent, outer[i - 2] = lax.optimization_barrier((sent, outer[i - 2]))
        for hop in range(half - 1):
            low, high = half - 1 - hop, half + hop
            got = lax.ppermute(sent, "dom", [(low, low - 1), (high, high + 1)])
            sent = jnp.where((at < low) | (at > high), got, sent)
        outer.append(sent)
    return [sent.astype(F32) for sent in outer]


ORDER = (6, 7, 4, 5, 2, 3, 1, 0)


def exchange(value_of, n_feat):
    got = []
    for k in ORDER[:-1]:
        got.append(lax.ppermute(value_of(k), "feat", [(i, i ^ k) for i in range(n_feat)]))
    return got + [value_of(0)]


def dense_body(
    n_dom,
    n_feat,
    features,
    proj_weight,
    source_block,
    slot_count,
    block_pattern,
    node_type,
    type_gain,
    cotangent,
):
    source_block = jnp.transpose(source_block, (1, 2, 0))
    slot_count = jnp.transpose(slot_count, (1, 0))
    inv_deg, pieces, adj = forward(
        features, proj_weight, source_block, slot_count, block_pattern, n_feat
    )
    received = exchange(lambda k: pieces[k], n_feat)
    x_t, col = transposed(features, inv_deg)
    activations, slope = combine(received, node_type, type_gain, cotangent)
    slopes = exchange(lambda k: slope, n_feat)
    chunks = [
        gradient(x_t, adj[relation], col[relation], slopes)
        for relation in range(proj_weight.shape[0])
    ]
    return activations, jnp.stack(chain_sum(chunks, n_dom))


def body(n_dom, n_feat, *args):
    nodes, relations = args[0].shape[0], args[2].shape[1]
    fits = 2 * relations * nodes * nodes <= 8 * MIB
    if fits and n_feat == 8 and n_dom % 2 == 0 and nodes == n_feat * BLK:
        return dense_body(n_dom, n_feat, *args)
    return general_body(*args)


def solution(mesh):
    placed = (
        P("dom", "feat"),
        P(None, "feat", None),
        P("dom", None, None),
        P("dom", None),
        P("dom", None, None, None, None),
        P(("dom", "feat")),
        P(),
        P(("dom", "feat"), None),
    )
    return jax.shard_map(
        functools.partial(body, mesh.shape["dom"], mesh.shape["feat"]),
        mesh=mesh,
        in_specs=placed,
        out_specs=(P(("dom", "feat"), None), P(None, "feat", None)),
        check_vma=False,
    )
```

```python
import functools

import jax
import jax.numpy as jnp
from jax import lax
from jax.experimental import pallas as pl
from jax.experimental.pallas import tpu as pltpu
from jax.sharding import PartitionSpec as P

BLK = 128
MIB = 1024 * 1024
BF16 = jnp.bfloat16
F32 = jnp.float32


def unpack_bits(packed):
    shifts = (2 ** jnp.arange(16)).astype(jnp.int32)
    bit_values = packed[..., None] // shifts % 2
    bit_values = jnp.swapaxes(bit_values, -3, -2)
    return bit_values.reshape(packed.shape[:-2] + (packed.shape[-1], packed.shape[-2] * 16))


def silu_grad(pre_act):
    sigmoid_value = jax.nn.sigmoid(pre_act)
    return sigmoid_value * (1.0 + pre_act * (1.0 - sigmoid_value))


def type_rows(node_type, type_gain):
    onehot = (
        node_type[:, None] == jnp.arange(type_gain.shape[0], dtype=jnp.int32)[None, :]
    ).astype(jnp.float32)
    return jnp.sum(onehot[:, :, None] * type_gain[None, :, :], axis=1)


def aggregate(features, source_block, slot_count, block_pattern):
    count_blocks = source_block.shape[0]
    relations = source_block.shape[1]
    slots_each = source_block.shape[2]
    col_width = features.shape[1]
    blocks = features.reshape(count_blocks, BLK, col_width)
    blocks_wide = blocks.astype(jnp.float32)
    live_slots = (
        jnp.arange(slots_each, dtype=jnp.int32)[None, None, :] < slot_count[:, :, None]
    ).astype(jnp.float32)
    mixed_list = []
    for relation in range(relations):
        summed = jnp.zeros((count_blocks, BLK, col_width), jnp.float32)
        degree = jnp.zeros((count_blocks, BLK), jnp.float32)
        for slot_index in range(slots_each):
            adjacency = (
                unpack_bits(block_pattern[:, relation, slot_index]).astype(jnp.float32)
                * live_slots[:, relation, slot_index][:, None, None]
            )
            picked = jnp.take(blocks, source_block[:, relation, slot_index], axis=0)
            summed = summed + jnp.einsum(
                "bij,bjc->bic",
                adjacency.astype(jnp.bfloat16),
                picked,
                preferred_element_type=jnp.float32,
            )
            degree = degree + jnp.sum(adjacency, axis=2)
        mixed_rows = ((blocks_wide + summed) / (1.0 + degree)[:, :, None]).astype(jnp.bfloat16)
        mixed_list.append(mixed_rows.reshape(count_blocks * BLK, col_width))
    return jnp.stack(mixed_list)


def general_body(
    features, proj_weight, source_block, slot_count, block_pattern, node_type, type_gain, cotangent
):
    mixed_all = aggregate(features, source_block, slot_count, block_pattern)
    pre_act = lax.psum_scatter(
        jnp.einsum("rnc,rch->nh", mixed_all, proj_weight, preferred_element_type=jnp.float32),
        "feat",
        scatter_dimension=0,
        tiled=True,
    )
    row_gains = type_rows(node_type, type_gain)
    output = (jax.nn.silu(pre_act) * row_gains).astype(jnp.bfloat16)
    slope_rows = (cotangent.astype(jnp.float32) * row_gains * silu_grad(pre_act)).astype(
        jnp.bfloat16
    )
    local_grad = jnp.einsum(
        "rnc,nh->rch",
        mixed_all,
        lax.all_gather(slope_rows, "feat", axis=0, tiled=True),
        preferred_element_type=jnp.float32,
    )
    weight_grad = lax.psum(local_grad, "dom")
    return (output, weight_grad)


def live_words(relation, slot, b, cnt_ref, pat_ref):
    live = jnp.where(slot < cnt_ref[relation, b], 0xFFFF, 0)
    return pat_ref[b, relation, slot] & live


def start_adjacency(places):
    sub = lax.broadcasted_iota(jnp.int32, (BLK, BLK), 0)
    lane = lax.broadcasted_iota(jnp.int32, (BLK, BLK), 1)
    eye = jnp.where(sub == lane, 1.0, 0.0).astype(BF16)
    for b, (ref, lanes) in enumerate(places):
        ref[:, lanes] = jnp.zeros((ref.shape[0], BLK), BF16)
        ref[b * BLK : (b + 1) * BLK, lanes] = eye


def add_edges(relation, places, src_ref, cnt_ref, pat_ref):
    bit = jnp.left_shift(1, lax.broadcasted_iota(jnp.int32, (16, BLK), 0))
    for s in range(src_ref.shape[1]):
        for b, (ref, lanes) in enumerate(places):
            words = live_words(relation, s, b, cnt_ref, pat_ref)
            row0 = pl.multiple_of(src_ref[relation, s, b] * BLK, BLK)
            parts = [
                jnp.where((words[w : w + 1, :] & bit) != 0, 1.0, 0.0)
                for w in range(words.shape[0])
            ]
            ref[pl.ds(row0, BLK), lanes] += jnp.concatenate(parts, axis=0).astype(BF16)


def inverse_degrees(relation, inv_ref, src_ref, cnt_ref, pat_ref):
    for b in range(src_ref.shape[2]):
        degree = jnp.zeros((8, BLK), jnp.int32)
        for s in range(src_ref.shape[1]):
            words = live_words(relation, s, b, cnt_ref, pat_ref)
            c = words - ((words >> 1) & 0x5555)
            c = (c & 0x3333) + ((c >> 2) & 0x3333)
            c = (c + (c >> 4)) & 0x0F0F
            degree = degree + ((c + (c >> 8)) & 0x1F)
        total = jnp.sum(degree.astype(F32), axis=0, keepdims=True)
        inv_ref[relation, 0:1, b * BLK : (b + 1) * BLK] = 1.0 / (1.0 + total)


def adjacency_kernel(src_ref, cnt_ref, pat_ref, inv_ref, *adj_refs):
    blocks = src_ref.shape[2]
    for relation, adj_ref in enumerate(adj_refs):
        places = [(adj_ref, slice(b * BLK, (b + 1) * BLK)) for b in range(blocks)]
        start_adjacency(places)
        inverse_degrees(relation, inv_ref, src_ref, cnt_ref, pat_ref)
        add_edges(relation, places, src_ref, cnt_ref, pat_ref)


def adjacency(source_block, slot_count, block_pattern):
    relations, _, blocks = source_block.shape
    nodes = blocks * BLK
    smem = pl.BlockSpec(memory_space=pltpu.SMEM)
    vmem = pl.BlockSpec(memory_space=pltpu.VMEM)
    inv_deg, *adj = pl.pallas_call(
        adjacency_kernel,
        name="adjacency",
        out_shape=[jax.ShapeDtypeStruct((relations, 8, nodes), F32)]
        + [jax.ShapeDtypeStruct((nodes, nodes), BF16)] * relations,
        in_specs=[smem, smem, vmem],
        out_specs=[vmem] * (1 + relations),
        compiler_params=pltpu.CompilerParams(vmem_limit_bytes=16 * MIB),
        cost_estimate=pl.CostEstimate(
            flops=1000 * relations * nodes * nodes,
            bytes_accessed=2 * relations * nodes * nodes,
            transcendentals=0,
        ),
    )(source_block, slot_count, block_pattern)
    return inv_deg, adj


def forward_kernel(n_feat, relations, inv_ref, *refs):
    adj_refs, refs = refs[:relations], refs[relations:]
    x_ref, w_ref, piece_refs, pre_ref = refs[0], refs[1], refs[2:-1], refs[-1]
    for relation in range(relations):
        y_t = lax.dot_general(
            w_ref[relation].T, x_ref[...], (((1,), (1,)), ((), ())), preferred_element_type=F32
        ).astype(BF16)
        p_t = jnp.dot(y_t, adj_refs[relation][...], preferred_element_type=F32)
        p_t = p_t * inv_ref[relation, 0:1, :]
        if relation == 0:
            pre_ref[...] = p_t
        else:
            pre_ref[...] += p_t

    me = lax.axis_index("feat")
    for k, piece in enumerate(piece_refs):
        first = pl.multiple_of((me ^ k) * BLK, BLK)
        piece[...] = pre_ref[:, pl.ds(first, BLK)].T.astype(BF16)


def forward(inv_deg, adj, features, proj_weight, n_feat):
    nodes, cols = features.shape
    relations, _, hidden = proj_weight.shape
    vmem = pl.BlockSpec(memory_space=pltpu.VMEM)
    return pl.pallas_call(
        functools.partial(forward_kernel, n_feat, relations),
        name="forward",
        out_shape=[jax.ShapeDtypeStruct((nodes // n_feat, hidden), BF16)] * n_feat,
        in_specs=[vmem] * (3 + relations),
        out_specs=[vmem] * n_feat,
        scratch_shapes=[pltpu.VMEM((hidden, nodes), F32)],
        compiler_params=pltpu.CompilerParams(vmem_limit_bytes=16 * MIB),
        cost_estimate=pl.CostEstimate(
            flops=2 * relations * nodes * hidden * (nodes + cols),
            bytes_accessed=2 * relations * nodes * nodes,
            transcendentals=0,
        ),
    )(inv_deg, *adj, features, proj_weight)


def transposed_kernel(x_ref, inv_ref, xt_ref, *col_refs):
    nodes = x_ref.shape[0]
    for b in range(nodes // BLK):
        rows = slice(b * BLK, (b + 1) * BLK)
        xt_ref[:, rows] = x_ref[rows, :].T
        for r, col_ref in enumerate(col_refs):
            wide = jnp.broadcast_to(inv_ref[r, 0:1, rows], (BLK, BLK))
            col_ref[rows, :] = wide.T


def transposed(features, inv_deg):
    nodes, cols = features.shape
    relations = inv_deg.shape[0]
    x_t, *col = pl.pallas_call(
        transposed_kernel,
        name="transposed",
        out_shape=[jax.ShapeDtypeStruct((cols, nodes), BF16)]
        + [jax.ShapeDtypeStruct((nodes, BLK), F32)] * relations,
        compiler_params=pltpu.CompilerParams(vmem_limit_bytes=8 * MIB),
        cost_estimate=pl.CostEstimate(
            flops=2 * nodes * cols, bytes_accessed=6 * nodes * cols, transcendentals=0
        ),
    )(features, inv_deg)
    return x_t, col


def combine_kernel(n_feat, *refs):
    type_ref, gain_ref, cot_ref, act_ref, slope_ref = refs[n_feat:]
    rows = act_ref.shape[0]
    pre = refs[0][...].astype(F32)
    for piece in refs[1:n_feat]:
        pre = pre + piece[...].astype(F32)
    types = jnp.broadcast_to(type_ref[...].astype(F32), (rows, rows)).T
    types = jnp.concatenate([types] * (act_ref.shape[1] // rows), axis=1)
    gain = jnp.zeros(act_ref.shape, F32)
    for t in range(gain_ref.shape[0]):
        gain = jnp.where(types == t, gain_ref[t : t + 1, :], gain)
    sig = jax.nn.sigmoid(pre)
    act_ref[...] = (pre * sig * gain).astype(BF16)
    grad = sig * (1.0 + pre * (1.0 - sig))
    slope_ref[...] = (cot_ref[...].astype(F32) * gain * grad).astype(BF16)


def combine(pieces, node_type, type_gain, cotangent):
    return pl.pallas_call(
        functools.partial(combine_kernel, len(pieces)),
        name="combine",
        out_shape=[jax.ShapeDtypeStruct(cotangent.shape, BF16)] * 2,
        compiler_params=pltpu.CompilerParams(vmem_limit_bytes=6 * MIB),
    )(*pieces, node_type[None, :], type_gain, cotangent)


def gradient_kernel(n_feat, xt_ref, adj_ref, col_ref, *rest):
    sent_refs, scaled_ref = rest[n_feat:-1], rest[-1]
    me = lax.axis_index("feat")
    for k, piece in zip(ORDER, rest[:n_feat]):
        rows = pl.ds(pl.multiple_of((me ^ k) * BLK, BLK), BLK)
        inv = jnp.concatenate([col_ref[rows, :]] * (piece.shape[1] // BLK), axis=1)
        scaled_ref[rows, :] = (piece[...].astype(F32) * inv).astype(BF16)
    spread = jnp.dot(adj_ref[...], scaled_ref[...], preferred_element_type=F32).astype(BF16)
    rows = xt_ref.shape[0] // len(sent_refs)
    for i, sent_ref in enumerate(sent_refs):
        x_t = xt_ref[i * rows : (i + 1) * rows, :]
        sent_ref[...] = jnp.dot(x_t, spread, preferred_element_type=F32).astype(BF16)


def gradient(parts, x_t, adj, col, slopes):
    cols, nodes = x_t.shape
    hidden = slopes[0].shape[1]
    vmem = pl.BlockSpec(memory_space=pltpu.VMEM)
    return pl.pallas_call(
        functools.partial(gradient_kernel, len(slopes)),
        name="gradient",
        out_shape=[jax.ShapeDtypeStruct((cols // parts, hidden), BF16)] * parts,
        in_specs=[vmem] * (3 + len(slopes)),
        out_specs=[vmem] * parts,
        scratch_shapes=[pltpu.VMEM((nodes, hidden), BF16)],
        compiler_params=pltpu.CompilerParams(vmem_limit_bytes=8 * MIB),
        cost_estimate=pl.CostEstimate(
            flops=2 * nodes * hidden * (nodes + cols),
            bytes_accessed=2 * nodes * nodes + 6 * cols * hidden,
            transcendentals=0,
        ),
    )(x_t, adj, col, *slopes)


def finish_kernel(n_dom, got_ref, sent_ref, *rest):
    at = lax.axis_index("dom")
    received = jnp.where((at == 0) | (at == n_dom - 1), 1.0, 0.0)
    got, sent = got_ref[...].astype(F32), sent_ref[...].astype(F32)
    rest[-1][0] = jnp.where(jnp.full(got.shape, received) > 0.5, got, sent)


def finish(place, shape, n_dom, got, sent, out):
    rows, cols = got.shape
    block = pl.BlockSpec((rows, cols), lambda i: (0, 0))
    before = [] if out is None else [out]
    return pl.pallas_call(
        functools.partial(finish_kernel, n_dom),
        name="finish",
        grid=(1,),
        out_shape=jax.ShapeDtypeStruct(shape, F32),
        in_specs=[block, block] + [pl.BlockSpec(memory_space=pl.ANY)] * len(before),
        out_specs=pl.BlockSpec((1, rows, cols), lambda i: (*place, 0)),
        input_output_aliases={2: 0} if before else {},
        compiler_params=pltpu.CompilerParams(vmem_limit_bytes=8 * MIB),
        cost_estimate=pl.CostEstimate(
            flops=2000000000, bytes_accessed=8 * rows * cols, transcendentals=0
        ),
    )(got, sent, *before)


def rounded(x):
    return lax.reduce_precision(x, 8, 7)


def chain_sum(chunks, n_dom, shape):
    half = n_dom // 2
    at = lax.axis_index("dom")
    inner = []
    for _, sent in chunks:
        for hop in range(half - 1):
            perm = [(hop, hop + 1), (n_dom - 1 - hop, n_dom - 2 - hop)]
            got = lax.ppermute(sent, "dom", perm)
            sent = rounded(sent.astype(F32) + got.astype(F32)).astype(BF16)
        inner.append(sent)
    middle = []
    for i, sent in enumerate(inner):
        if i >= 2:
            sent, _ = lax.optimization_barrier((sent, middle[i - 2]))
        got = lax.ppermute(sent, "dom", [(half - 1, half), (half, half - 1)])
        middle.append(rounded(sent.astype(F32) + got.astype(F32)).astype(BF16))
    out = None
    for i, sent in enumerate(middle):
        got = sent
        for hop in range(half - 1):
            low, high = half - 1 - hop, half + hop
            if hop:
                sent = jnp.where((at < low + 1) | (at > high - 1), got, sent)
            got = lax.ppermute(sent, "dom", [(low, low - 1), (high, high + 1)])
        out = finish(chunks[i][0], shape, n_dom, got, sent, out)
    return out


ORDER = (6, 7, 4, 5, 2, 3, 1, 0)


def exchange(value_of, n_feat):
    got = []
    for k in ORDER[:-1]:
        got.append(lax.ppermute(value_of(k), "feat", [(i, i ^ k) for i in range(n_feat)]))
    return got + [value_of(0)]


def dense_body(
    n_dom,
    n_feat,
    features,
    proj_weight,
    source_block,
    slot_count,
    block_pattern,
    node_type,
    type_gain,
    cotangent,
):
    source_block = jnp.transpose(source_block, (1, 2, 0))
    slot_count = jnp.transpose(slot_count, (1, 0))
    inv_deg, adj = adjacency(source_block, slot_count, block_pattern)
    pieces = forward(inv_deg, adj, features, proj_weight, n_feat)
    received = exchange(lambda k: pieces[k], n_feat)
    x_t, col = transposed(features, inv_deg)
    activations, slope = combine(received, node_type, type_gain, cotangent)
    slopes = exchange(lambda k: slope, n_feat)
    chunks = []
    for relation in range(proj_weight.shape[0]):
        parts = 2 if relation == 0 else 1
        made = gradient(parts, x_t, adj[relation], col[relation], slopes)
        chunks += [((relation, i), chunk) for i, chunk in enumerate(made)]
    shape = (proj_weight.shape[0], features.shape[1], proj_weight.shape[2])
    return activations, chain_sum(chunks, n_dom, shape)


def body(n_dom, n_feat, *args):
    nodes, relations = args[0].shape[0], args[2].shape[1]
    fits = 2 * relations * nodes * nodes <= 8 * MIB
    if fits and n_feat == 8 and n_dom % 2 == 0 and nodes == n_feat * BLK:
        return dense_body(n_dom, n_feat, *args)
    return general_body(*args)


def solution(mesh):
    placed = (
        P("dom", "feat"),
        P(None, "feat", None),
        P("dom", None, None),
        P("dom", None),
        P("dom", None, None, None, None),
        P(("dom", "feat")),
        P(),
        P(("dom", "feat"), None),
    )
    return jax.shard_map(
        functools.partial(body, mesh.shape["dom"], mesh.shape["feat"]),
        mesh=mesh,
        in_specs=placed,
        out_specs=(P(("dom", "feat"), None), P(None, "feat", None)),
        check_vma=False,
    )
```

```python
import functools

import jax
import jax.numpy as jnp
from jax import lax
from jax.experimental import pallas as pl
from jax.experimental.pallas import tpu as pltpu
from jax.sharding import PartitionSpec as P

BLK = 128
MIB = 1024 * 1024
BF16 = jnp.bfloat16
F32 = jnp.float32


def unpack_bits(packed):
    shifts = (2 ** jnp.arange(16)).astype(jnp.int32)
    bit_values = packed[..., None] // shifts % 2
    bit_values = jnp.swapaxes(bit_values, -3, -2)
    return bit_values.reshape(packed.shape[:-2] + (packed.shape[-1], packed.shape[-2] * 16))


def silu_grad(pre_act):
    sigmoid_value = jax.nn.sigmoid(pre_act)
    return sigmoid_value * (1.0 + pre_act * (1.0 - sigmoid_value))


def type_rows(node_type, type_gain):
    onehot = (
        node_type[:, None] == jnp.arange(type_gain.shape[0], dtype=jnp.int32)[None, :]
    ).astype(jnp.float32)
    return jnp.sum(onehot[:, :, None] * type_gain[None, :, :], axis=1)


def aggregate(features, source_block, slot_count, block_pattern):
    count_blocks = source_block.shape[0]
    relations = source_block.shape[1]
    slots_each = source_block.shape[2]
    col_width = features.shape[1]
    blocks = features.reshape(count_blocks, BLK, col_width)
    blocks_wide = blocks.astype(jnp.float32)
    live_slots = (
        jnp.arange(slots_each, dtype=jnp.int32)[None, None, :] < slot_count[:, :, None]
    ).astype(jnp.float32)
    mixed_list = []
    for relation in range(relations):
        summed = jnp.zeros((count_blocks, BLK, col_width), jnp.float32)
        degree = jnp.zeros((count_blocks, BLK), jnp.float32)
        for slot_index in range(slots_each):
            adjacency = (
                unpack_bits(block_pattern[:, relation, slot_index]).astype(jnp.float32)
                * live_slots[:, relation, slot_index][:, None, None]
            )
            picked = jnp.take(blocks, source_block[:, relation, slot_index], axis=0)
            summed = summed + jnp.einsum(
                "bij,bjc->bic",
                adjacency.astype(jnp.bfloat16),
                picked,
                preferred_element_type=jnp.float32,
            )
            degree = degree + jnp.sum(adjacency, axis=2)
        mixed_rows = ((blocks_wide + summed) / (1.0 + degree)[:, :, None]).astype(jnp.bfloat16)
        mixed_list.append(mixed_rows.reshape(count_blocks * BLK, col_width))
    return jnp.stack(mixed_list)


def general_body(
    features, proj_weight, source_block, slot_count, block_pattern, node_type, type_gain, cotangent
):
    mixed_all = aggregate(features, source_block, slot_count, block_pattern)
    pre_act = lax.psum_scatter(
        jnp.einsum("rnc,rch->nh", mixed_all, proj_weight, preferred_element_type=jnp.float32),
        "feat",
        scatter_dimension=0,
        tiled=True,
    )
    row_gains = type_rows(node_type, type_gain)
    output = (jax.nn.silu(pre_act) * row_gains).astype(jnp.bfloat16)
    slope_rows = (cotangent.astype(jnp.float32) * row_gains * silu_grad(pre_act)).astype(
        jnp.bfloat16
    )
    local_grad = jnp.einsum(
        "rnc,nh->rch",
        mixed_all,
        lax.all_gather(slope_rows, "feat", axis=0, tiled=True),
        preferred_element_type=jnp.float32,
    )
    weight_grad = lax.psum(local_grad, "dom")
    return (output, weight_grad)


def live_words(relation, slot, b, cnt_ref, pat_ref):
    live = jnp.where(slot < cnt_ref[relation, b], 0xFFFF, 0)
    return pat_ref[b, relation, slot] & live


def start_adjacency(places):
    sub = lax.broadcasted_iota(jnp.int32, (BLK, BLK), 0)
    lane = lax.broadcasted_iota(jnp.int32, (BLK, BLK), 1)
    eye = jnp.where(sub == lane, 1.0, 0.0).astype(BF16)
    for b, (ref, lanes) in enumerate(places):
        ref[:, lanes] = jnp.zeros((ref.shape[0], BLK), BF16)
        ref[b * BLK : (b + 1) * BLK, lanes] = eye


def add_edges(relation, places, src_ref, cnt_ref, pat_ref):
    bit = jnp.left_shift(1, lax.broadcasted_iota(jnp.int32, (16, BLK), 0))
    for s in range(src_ref.shape[1]):
        for b, (ref, lanes) in enumerate(places):
            words = live_words(relation, s, b, cnt_ref, pat_ref)
            row0 = pl.multiple_of(src_ref[relation, s, b] * BLK, BLK)
            parts = [
                jnp.where((words[w : w + 1, :] & bit) != 0, 1.0, 0.0)
                for w in range(words.shape[0])
            ]
            ref[pl.ds(row0, BLK), lanes] += jnp.concatenate(parts, axis=0).astype(BF16)


def inverse_degrees(relation, inv_ref, src_ref, cnt_ref, pat_ref):
    for b in range(src_ref.shape[2]):
        degree = jnp.zeros((8, BLK), jnp.int32)
        for s in range(src_ref.shape[1]):
            words = live_words(relation, s, b, cnt_ref, pat_ref)
            c = words - ((words >> 1) & 0x5555)
            c = (c & 0x3333) + ((c >> 2) & 0x3333)
            c = (c + (c >> 4)) & 0x0F0F
            degree = degree + ((c + (c >> 8)) & 0x1F)
        total = jnp.sum(degree.astype(F32), axis=0, keepdims=True)
        inv_ref[relation, 0:1, b * BLK : (b + 1) * BLK] = 1.0 / (1.0 + total)


def adjacency_kernel(src_ref, cnt_ref, pat_ref, inv_ref, *adj_refs):
    blocks = src_ref.shape[2]
    for relation, adj_ref in enumerate(adj_refs):
        places = [(adj_ref, slice(b * BLK, (b + 1) * BLK)) for b in range(blocks)]
        start_adjacency(places)
        inverse_degrees(relation, inv_ref, src_ref, cnt_ref, pat_ref)
        add_edges(relation, places, src_ref, cnt_ref, pat_ref)


def adjacency(source_block, slot_count, block_pattern):
    relations, _, blocks = source_block.shape
    nodes = blocks * BLK
    smem = pl.BlockSpec(memory_space=pltpu.SMEM)
    vmem = pl.BlockSpec(memory_space=pltpu.VMEM)
    inv_deg, *adj = pl.pallas_call(
        adjacency_kernel,
        name="adjacency",
        out_shape=[jax.ShapeDtypeStruct((relations, 8, nodes), F32)]
        + [jax.ShapeDtypeStruct((nodes, nodes), BF16)] * relations,
        in_specs=[smem, smem, vmem],
        out_specs=[vmem] * (1 + relations),
        compiler_params=pltpu.CompilerParams(vmem_limit_bytes=16 * MIB),
        cost_estimate=pl.CostEstimate(
            flops=1000 * relations * nodes * nodes,
            bytes_accessed=2 * relations * nodes * nodes,
            transcendentals=0,
        ),
    )(source_block, slot_count, block_pattern)
    return inv_deg, adj


def forward_kernel(n_feat, relations, inv_ref, *refs):
    adj_refs, refs = refs[:relations], refs[relations:]
    x_ref, w_ref, piece_refs, pre_ref = refs[0], refs[1], refs[2:-1], refs[-1]
    for relation in range(relations):
        y_t = lax.dot_general(
            w_ref[relation].T, x_ref[...], (((1,), (1,)), ((), ())), preferred_element_type=F32
        ).astype(BF16)
        p_t = jnp.dot(y_t, adj_refs[relation][...], preferred_element_type=F32)
        p_t = p_t * inv_ref[relation, 0:1, :]
        if relation == 0:
            pre_ref[...] = p_t
        else:
            pre_ref[...] += p_t

    me = lax.axis_index("feat")
    for k, piece in enumerate(piece_refs):
        first = pl.multiple_of((me ^ k) * BLK, BLK)
        piece[...] = pre_ref[:, pl.ds(first, BLK)].T.astype(piece.dtype)


def forward(inv_deg, adj, features, proj_weight, n_feat):
    nodes, cols = features.shape
    relations, _, hidden = proj_weight.shape
    vmem = pl.BlockSpec(memory_space=pltpu.VMEM)
    return pl.pallas_call(
        functools.partial(forward_kernel, n_feat, relations),
        name="forward",
        out_shape=[
            jax.ShapeDtypeStruct((nodes // n_feat, hidden), BF16 if k % 2 else F32)
            for k in range(n_feat)
        ],
        in_specs=[vmem] * (3 + relations),
        out_specs=[vmem] * n_feat,
        scratch_shapes=[pltpu.VMEM((hidden, nodes), F32)],
        compiler_params=pltpu.CompilerParams(vmem_limit_bytes=16 * MIB),
        cost_estimate=pl.CostEstimate(
            flops=2 * relations * nodes * hidden * (nodes + cols),
            bytes_accessed=2 * relations * nodes * nodes,
            transcendentals=0,
        ),
    )(inv_deg, *adj, features, proj_weight)


def transposed_kernel(x_ref, inv_ref, xt_ref, *col_refs):
    nodes = x_ref.shape[0]
    for b in range(nodes // BLK):
        rows = slice(b * BLK, (b + 1) * BLK)
        xt_ref[:, rows] = x_ref[rows, :].T
        for r, col_ref in enumerate(col_refs):
            wide = jnp.broadcast_to(inv_ref[r, 0:1, rows], (BLK, BLK))
            col_ref[rows, :] = wide.T


def transposed(features, inv_deg):
    nodes, cols = features.shape
    relations = inv_deg.shape[0]
    x_t, *col = pl.pallas_call(
        transposed_kernel,
        name="transposed",
        out_shape=[jax.ShapeDtypeStruct((cols, nodes), BF16)]
        + [jax.ShapeDtypeStruct((nodes, BLK), F32)] * relations,
        compiler_params=pltpu.CompilerParams(vmem_limit_bytes=8 * MIB),
        cost_estimate=pl.CostEstimate(
            flops=2 * nodes * cols, bytes_accessed=6 * nodes * cols, transcendentals=0
        ),
    )(features, inv_deg)
    return x_t, col


def combine_kernel(n_feat, *refs):
    type_ref, gain_ref, cot_ref, act_ref, slope_ref = refs[n_feat:]
    rows = act_ref.shape[0]
    pre = refs[0][...].astype(F32)
    for piece in refs[1:n_feat]:
        pre = pre + piece[...].astype(F32)
    types = jnp.broadcast_to(type_ref[...].astype(F32), (rows, rows)).T
    types = jnp.concatenate([types] * (act_ref.shape[1] // rows), axis=1)
    gain = jnp.zeros(act_ref.shape, F32)
    for t in range(gain_ref.shape[0]):
        gain = jnp.where(types == t, gain_ref[t : t + 1, :], gain)
    sig = jax.nn.sigmoid(pre)
    act_ref[...] = (pre * sig * gain).astype(BF16)
    grad = sig * (1.0 + pre * (1.0 - sig))
    slope_ref[...] = (cot_ref[...].astype(F32) * gain * grad).astype(BF16)


def combine(pieces, node_type, type_gain, cotangent):
    return pl.pallas_call(
        functools.partial(combine_kernel, len(pieces)),
        name="combine",
        out_shape=[jax.ShapeDtypeStruct(cotangent.shape, BF16)] * 2,
        compiler_params=pltpu.CompilerParams(vmem_limit_bytes=6 * MIB),
    )(*pieces, node_type[None, :], type_gain, cotangent)


def gradient_kernel(n_feat, xt_ref, adj_ref, col_ref, *rest):
    sent_refs, scaled_ref = rest[n_feat:-1], rest[-1]
    me = lax.axis_index("feat")
    for k, piece in zip(ORDER, rest[:n_feat]):
        rows = pl.ds(pl.multiple_of((me ^ k) * BLK, BLK), BLK)
        inv = jnp.concatenate([col_ref[rows, :]] * (piece.shape[1] // BLK), axis=1)
        scaled_ref[rows, :] = (piece[...].astype(F32) * inv).astype(BF16)
    spread = jnp.dot(adj_ref[...], scaled_ref[...], preferred_element_type=F32).astype(BF16)
    rows = xt_ref.shape[0] // len(sent_refs)
    for i, sent_ref in enumerate(sent_refs):
        x_t = xt_ref[i * rows : (i + 1) * rows, :]
        sent_ref[...] = jnp.dot(x_t, spread, preferred_element_type=F32).astype(BF16)


def gradient(parts, x_t, adj, col, slopes):
    cols, nodes = x_t.shape
    hidden = slopes[0].shape[1]
    vmem = pl.BlockSpec(memory_space=pltpu.VMEM)
    return pl.pallas_call(
        functools.partial(gradient_kernel, len(slopes)),
        name="gradient",
        out_shape=[jax.ShapeDtypeStruct((cols // parts, hidden), BF16)] * parts,
        in_specs=[vmem] * (3 + len(slopes)),
        out_specs=[vmem] * parts,
        scratch_shapes=[pltpu.VMEM((nodes, hidden), BF16)],
        compiler_params=pltpu.CompilerParams(vmem_limit_bytes=8 * MIB),
        cost_estimate=pl.CostEstimate(
            flops=2 * nodes * hidden * (nodes + cols),
            bytes_accessed=2 * nodes * nodes + 6 * cols * hidden,
            transcendentals=0,
        ),
    )(x_t, adj, col, *slopes)


def finish_kernel(n_dom, got_ref, sent_ref, *rest):
    at = lax.axis_index("dom")
    received = jnp.where((at == 0) | (at == n_dom - 1), 1.0, 0.0)
    got, sent = got_ref[...].astype(F32), sent_ref[...].astype(F32)
    rest[-1][0] = jnp.where(jnp.full(got.shape, received) > 0.5, got, sent)


def finish(place, shape, n_dom, got, sent, out):
    rows, cols = got.shape
    block = pl.BlockSpec((rows, cols), lambda i: (0, 0))
    before = [] if out is None else [out]
    return pl.pallas_call(
        functools.partial(finish_kernel, n_dom),
        name="finish",
        grid=(1,),
        out_shape=jax.ShapeDtypeStruct(shape, F32),
        in_specs=[block, block] + [pl.BlockSpec(memory_space=pl.ANY)] * len(before),
        out_specs=pl.BlockSpec((1, rows, cols), lambda i: (*place, 0)),
        input_output_aliases={2: 0} if before else {},
        compiler_params=pltpu.CompilerParams(vmem_limit_bytes=8 * MIB),
        cost_estimate=pl.CostEstimate(
            flops=2000000000, bytes_accessed=8 * rows * cols, transcendentals=0
        ),
    )(got, sent, *before)


def rounded(x):
    return lax.reduce_precision(x, 8, 7)


def chain_sum(chunks, n_dom, shape):
    half = n_dom // 2
    at = lax.axis_index("dom")
    inner = []
    for _, sent in chunks:
        for hop in range(half - 1):
            perm = [(hop, hop + 1), (n_dom - 1 - hop, n_dom - 2 - hop)]
            got = lax.ppermute(sent, "dom", perm)
            sent = rounded(sent.astype(F32) + got.astype(F32)).astype(BF16)
        inner.append(sent)
    middle = []
    for i, sent in enumerate(inner):
        if i >= 2:
            sent, _ = lax.optimization_barrier((sent, middle[i - 2]))
        got = lax.ppermute(sent, "dom", [(half - 1, half), (half, half - 1)])
        middle.append(rounded(sent.astype(F32) + got.astype(F32)).astype(BF16))
    out = None
    for i, sent in enumerate(middle):
        got = sent
        for hop in range(half - 1):
            low, high = half - 1 - hop, half + hop
            if hop:
                sent = jnp.where((at < low + 1) | (at > high - 1), got, sent)
            got = lax.ppermute(sent, "dom", [(low, low - 1), (high, high + 1)])
        out = finish(chunks[i][0], shape, n_dom, got, sent, out)
    return out


ORDER = (6, 4, 2, 0, 1, 3, 5, 7)


def swap(value, k, n_feat):
    return lax.ppermute(value, "feat", [(i, i ^ k) for i in range(n_feat)])


def reduce_pieces(pieces, n_feat):
    other = {k: swap(pieces[k + 1], 1, n_feat) for k in (6, 4, 2, 0)}
    terms = []
    for k in (6, 4, 2):
        chip = (pieces[k] + other[k].astype(F32)).astype(BF16)
        terms.append(swap(chip, k, n_feat))
    return terms + [other[0], pieces[0]]


def gather_pieces(piece, n_feat):
    got = {0: piece}
    for k in (6, 4, 2):
        got[k] = swap(piece, k, n_feat)
    for k in (0, 6, 4, 2):
        got[k + 1] = swap(got[k], 1, n_feat)
    return [got[k] for k in ORDER]


def dense_body(
    n_dom,
    n_feat,
    features,
    proj_weight,
    source_block,
    slot_count,
    block_pattern,
    node_type,
    type_gain,
    cotangent,
):
    source_block = jnp.transpose(source_block, (1, 2, 0))
    slot_count = jnp.transpose(slot_count, (1, 0))
    inv_deg, adj = adjacency(source_block, slot_count, block_pattern)
    pieces = forward(inv_deg, adj, features, proj_weight, n_feat)
    received = reduce_pieces(pieces, n_feat)
    x_t, col = transposed(features, inv_deg)
    activations, slope = combine(received, node_type, type_gain, cotangent)
    slopes = gather_pieces(slope, n_feat)
    chunks = []
    for relation in range(proj_weight.shape[0]):
        parts = 2 if relation == 0 else 1
        made = gradient(parts, x_t, adj[relation], col[relation], slopes)
        chunks += [((relation, i), chunk) for i, chunk in enumerate(made)]
    shape = (proj_weight.shape[0], features.shape[1], proj_weight.shape[2])
    return activations, chain_sum(chunks, n_dom, shape)


def body(n_dom, n_feat, *args):
    nodes, relations = args[0].shape[0], args[2].shape[1]
    fits = 2 * relations * nodes * nodes <= 8 * MIB
    if fits and n_feat == 8 and n_dom % 2 == 0 and nodes == n_feat * BLK:
        return dense_body(n_dom, n_feat, *args)
    return general_body(*args)


def solution(mesh):
    placed = (
        P("dom", "feat"),
        P(None, "feat", None),
        P("dom", None, None),
        P("dom", None),
        P("dom", None, None, None, None),
        P(("dom", "feat")),
        P(),
        P(("dom", "feat"), None),
    )
    return jax.shard_map(
        functools.partial(body, mesh.shape["dom"], mesh.shape["feat"]),
        mesh=mesh,
        in_specs=placed,
        out_specs=(P(("dom", "feat"), None), P(None, "feat", None)),
        check_vma=False,
    )
```

```python
import functools

import jax
import jax.numpy as jnp
from jax import lax
from jax.experimental import pallas as pl
from jax.experimental.pallas import tpu as pltpu
from jax.sharding import PartitionSpec as P

BLK = 128
MIB = 1024 * 1024
BF16 = jnp.bfloat16
F32 = jnp.float32


def unpack_bits(packed):
    shifts = (2 ** jnp.arange(16)).astype(jnp.int32)
    bit_values = packed[..., None] // shifts % 2
    bit_values = jnp.swapaxes(bit_values, -3, -2)
    return bit_values.reshape(packed.shape[:-2] + (packed.shape[-1], packed.shape[-2] * 16))


def silu_grad(pre_act):
    sigmoid_value = jax.nn.sigmoid(pre_act)
    return sigmoid_value * (1.0 + pre_act * (1.0 - sigmoid_value))


def type_rows(node_type, type_gain):
    onehot = (
        node_type[:, None] == jnp.arange(type_gain.shape[0], dtype=jnp.int32)[None, :]
    ).astype(jnp.float32)
    return jnp.sum(onehot[:, :, None] * type_gain[None, :, :], axis=1)


def aggregate(features, source_block, slot_count, block_pattern):
    count_blocks = source_block.shape[0]
    relations = source_block.shape[1]
    slots_each = source_block.shape[2]
    col_width = features.shape[1]
    blocks = features.reshape(count_blocks, BLK, col_width)
    blocks_wide = blocks.astype(jnp.float32)
    live_slots = (
        jnp.arange(slots_each, dtype=jnp.int32)[None, None, :] < slot_count[:, :, None]
    ).astype(jnp.float32)
    mixed_list = []
    for relation in range(relations):
        summed = jnp.zeros((count_blocks, BLK, col_width), jnp.float32)
        degree = jnp.zeros((count_blocks, BLK), jnp.float32)
        for slot_index in range(slots_each):
            adjacency = (
                unpack_bits(block_pattern[:, relation, slot_index]).astype(jnp.float32)
                * live_slots[:, relation, slot_index][:, None, None]
            )
            picked = jnp.take(blocks, source_block[:, relation, slot_index], axis=0)
            summed = summed + jnp.einsum(
                "bij,bjc->bic",
                adjacency.astype(jnp.bfloat16),
                picked,
                preferred_element_type=jnp.float32,
            )
            degree = degree + jnp.sum(adjacency, axis=2)
        mixed_rows = ((blocks_wide + summed) / (1.0 + degree)[:, :, None]).astype(jnp.bfloat16)
        mixed_list.append(mixed_rows.reshape(count_blocks * BLK, col_width))
    return jnp.stack(mixed_list)


def general_body(
    features, proj_weight, source_block, slot_count, block_pattern, node_type, type_gain, cotangent
):
    mixed_all = aggregate(features, source_block, slot_count, block_pattern)
    pre_act = lax.psum_scatter(
        jnp.einsum("rnc,rch->nh", mixed_all, proj_weight, preferred_element_type=jnp.float32),
        "feat",
        scatter_dimension=0,
        tiled=True,
    )
    row_gains = type_rows(node_type, type_gain)
    output = (jax.nn.silu(pre_act) * row_gains).astype(jnp.bfloat16)
    slope_rows = (cotangent.astype(jnp.float32) * row_gains * silu_grad(pre_act)).astype(
        jnp.bfloat16
    )
    local_grad = jnp.einsum(
        "rnc,nh->rch",
        mixed_all,
        lax.all_gather(slope_rows, "feat", axis=0, tiled=True),
        preferred_element_type=jnp.float32,
    )
    weight_grad = lax.psum(local_grad, "dom")
    return (output, weight_grad)


def live_words(relation, slot, b, cnt_ref, pat_ref):
    live = jnp.where(slot < cnt_ref[relation, b], 0xFFFF, 0)
    return pat_ref[b, relation, slot] & live


def start_adjacency(places):
    sub = lax.broadcasted_iota(jnp.int32, (BLK, BLK), 0)
    lane = lax.broadcasted_iota(jnp.int32, (BLK, BLK), 1)
    eye = jnp.where(sub == lane, 1.0, 0.0).astype(BF16)
    for b, (ref, lanes) in enumerate(places):
        ref[:, lanes] = jnp.zeros((ref.shape[0], BLK), BF16)
        ref[b * BLK : (b + 1) * BLK, lanes] = eye


def add_edges(relation, places, src_ref, cnt_ref, pat_ref):
    bit = jnp.left_shift(1, lax.broadcasted_iota(jnp.int32, (16, BLK), 0))
    group = 4
    for s in range(src_ref.shape[1]):
        for b0 in range(0, len(places), group):
            held = []
            for b in range(b0, min(b0 + group, len(places))):
                ref, lanes = places[b]
                row0 = pl.multiple_of(src_ref[relation, s, b] * BLK, BLK)
                held.append((ref, pl.ds(row0, BLK), lanes, ref[pl.ds(row0, BLK), lanes]))
            for b, (ref, rows, lanes, tile) in enumerate(held, b0):
                words = live_words(relation, s, b, cnt_ref, pat_ref)
                parts = [
                    jnp.where((words[w : w + 1, :] & bit) != 0, 1.0, 0.0)
                    for w in range(words.shape[0])
                ]
                ref[rows, lanes] = tile + jnp.concatenate(parts, axis=0).astype(BF16)


def inverse_degrees(relation, inv_ref, src_ref, cnt_ref, pat_ref):
    for b in range(src_ref.shape[2]):
        degree = jnp.zeros((8, BLK), jnp.int32)
        for s in range(src_ref.shape[1]):
            words = live_words(relation, s, b, cnt_ref, pat_ref)
            c = words - ((words >> 1) & 0x5555)
            c = (c & 0x3333) + ((c >> 2) & 0x3333)
            c = (c + (c >> 4)) & 0x0F0F
            degree = degree + ((c + (c >> 8)) & 0x1F)
        total = jnp.sum(degree.astype(F32), axis=0, keepdims=True)
        inv_ref[relation, 0:1, b * BLK : (b + 1) * BLK] = 1.0 / (1.0 + total)


def adjacency_kernel(src_ref, cnt_ref, pat_ref, inv_ref, *adj_refs):
    blocks = src_ref.shape[2]
    for relation, adj_ref in enumerate(adj_refs):
        places = [(adj_ref, slice(b * BLK, (b + 1) * BLK)) for b in range(blocks)]
        start_adjacency(places)
        inverse_degrees(relation, inv_ref, src_ref, cnt_ref, pat_ref)
        add_edges(relation, places, src_ref, cnt_ref, pat_ref)


def adjacency(source_block, slot_count, block_pattern):
    relations, _, blocks = source_block.shape
    nodes = blocks * BLK
    smem = pl.BlockSpec(memory_space=pltpu.SMEM)
    vmem = pl.BlockSpec(memory_space=pltpu.VMEM)
    inv_deg, *adj = pl.pallas_call(
        adjacency_kernel,
        name="adjacency",
        out_shape=[jax.ShapeDtypeStruct((relations, 8, nodes), F32)]
        + [jax.ShapeDtypeStruct((nodes, nodes), BF16)] * relations,
        in_specs=[smem, smem, vmem],
        out_specs=[vmem] * (1 + relations),
        compiler_params=pltpu.CompilerParams(vmem_limit_bytes=16 * MIB),
        cost_estimate=pl.CostEstimate(
            flops=1000 * relations * nodes * nodes,
            bytes_accessed=2 * relations * nodes * nodes,
            transcendentals=0,
        ),
    )(source_block, slot_count, block_pattern)
    return inv_deg, adj


def forward_kernel(n_feat, relations, inv_ref, *refs):
    adj_refs, refs = refs[:relations], refs[relations:]
    x_ref, w_ref, piece_refs, pre_ref = refs[0], refs[1], refs[2:-1], refs[-1]
    for relation in range(relations):
        y_t = lax.dot_general(
            w_ref[relation].T, x_ref[...], (((1,), (1,)), ((), ())), preferred_element_type=F32
        ).astype(BF16)
        p_t = jnp.dot(y_t, adj_refs[relation][...], preferred_element_type=F32)
        p_t = p_t * inv_ref[relation, 0:1, :]
        if relation == 0:
            pre_ref[...] = p_t
        else:
            pre_ref[...] += p_t

    me = lax.axis_index("feat")
    for k, piece in enumerate(piece_refs):
        first = pl.multiple_of((me ^ k) * BLK, BLK)
        piece[...] = pre_ref[:, pl.ds(first, BLK)].T.astype(piece.dtype)


def forward(inv_deg, adj, features, proj_weight, n_feat):
    nodes, cols = features.shape
    relations, _, hidden = proj_weight.shape
    vmem = pl.BlockSpec(memory_space=pltpu.VMEM)
    return pl.pallas_call(
        functools.partial(forward_kernel, n_feat, relations),
        name="forward",
        out_shape=[
            jax.ShapeDtypeStruct((nodes // n_feat, hidden), BF16 if k % 2 else F32)
            for k in range(n_feat)
        ],
        in_specs=[vmem] * (3 + relations),
        out_specs=[vmem] * n_feat,
        scratch_shapes=[pltpu.VMEM((hidden, nodes), F32)],
        compiler_params=pltpu.CompilerParams(vmem_limit_bytes=16 * MIB),
        cost_estimate=pl.CostEstimate(
            flops=2 * relations * nodes * hidden * (nodes + cols),
            bytes_accessed=2 * relations * nodes * nodes,
            transcendentals=0,
        ),
    )(inv_deg, *adj, features, proj_weight)


def transposed_kernel(x_ref, inv_ref, xt_ref, *col_refs):
    nodes = x_ref.shape[0]
    for b in range(nodes // BLK):
        rows = slice(b * BLK, (b + 1) * BLK)
        xt_ref[:, rows] = x_ref[rows, :].T
        for r, col_ref in enumerate(col_refs):
            wide = jnp.broadcast_to(inv_ref[r, 0:1, rows], (BLK, BLK))
            col_ref[rows, :] = wide.T


def transposed(features, inv_deg):
    nodes, cols = features.shape
    relations = inv_deg.shape[0]
    x_t, *col = pl.pallas_call(
        transposed_kernel,
        name="transposed",
        out_shape=[jax.ShapeDtypeStruct((cols, nodes), BF16)]
        + [jax.ShapeDtypeStruct((nodes, BLK), F32)] * relations,
        compiler_params=pltpu.CompilerParams(vmem_limit_bytes=8 * MIB),
        cost_estimate=pl.CostEstimate(
            flops=2 * nodes * cols, bytes_accessed=6 * nodes * cols, transcendentals=0
        ),
    )(features, inv_deg)
    return x_t, col


def combine_kernel(n_feat, *refs):
    type_ref, gain_ref, cot_ref, act_ref, slope_ref = refs[n_feat:]
    rows = act_ref.shape[0]
    pre = refs[0][...].astype(F32)
    for piece in refs[1:n_feat]:
        pre = pre + piece[...].astype(F32)
    types = jnp.broadcast_to(type_ref[...].astype(F32), (rows, rows)).T
    types = jnp.concatenate([types] * (act_ref.shape[1] // rows), axis=1)
    gain = jnp.zeros(act_ref.shape, F32)
    for t in range(gain_ref.shape[0]):
        gain = jnp.where(types == t, gain_ref[t : t + 1, :], gain)
    sig = jax.nn.sigmoid(pre)
    act_ref[...] = (pre * sig * gain).astype(BF16)
    grad = sig * (1.0 + pre * (1.0 - sig))
    slope_ref[...] = (cot_ref[...].astype(F32) * gain * grad).astype(BF16)


def combine(pieces, node_type, type_gain, cotangent):
    return pl.pallas_call(
        functools.partial(combine_kernel, len(pieces)),
        name="combine",
        out_shape=[jax.ShapeDtypeStruct(cotangent.shape, BF16)] * 2,
        compiler_params=pltpu.CompilerParams(vmem_limit_bytes=6 * MIB),
    )(*pieces, node_type[None, :], type_gain, cotangent)


def gradient_kernel(n_feat, xt_ref, adj_ref, col_ref, *rest):
    sent_refs, scaled_ref = rest[n_feat:-1], rest[-1]
    me = lax.axis_index("feat")
    for k, piece in zip(ORDER, rest[:n_feat]):
        rows = pl.ds(pl.multiple_of((me ^ k) * BLK, BLK), BLK)
        inv = jnp.concatenate([col_ref[rows, :]] * (piece.shape[1] // BLK), axis=1)
        scaled_ref[rows, :] = (piece[...].astype(F32) * inv).astype(BF16)
    spread = jnp.dot(adj_ref[...], scaled_ref[...], preferred_element_type=F32).astype(BF16)
    rows = xt_ref.shape[0] // len(sent_refs)
    for i, sent_ref in enumerate(sent_refs):
        x_t = xt_ref[i * rows : (i + 1) * rows, :]
        sent_ref[...] = jnp.dot(x_t, spread, preferred_element_type=F32).astype(BF16)


def gradient(parts, x_t, adj, col, slopes):
    cols, nodes = x_t.shape
    hidden = slopes[0].shape[1]
    vmem = pl.BlockSpec(memory_space=pltpu.VMEM)
    return pl.pallas_call(
        functools.partial(gradient_kernel, len(slopes)),
        name="gradient",
        out_shape=[jax.ShapeDtypeStruct((cols // parts, hidden), BF16)] * parts,
        in_specs=[vmem] * (3 + len(slopes)),
        out_specs=[vmem] * parts,
        scratch_shapes=[pltpu.VMEM((nodes, hidden), BF16)],
        compiler_params=pltpu.CompilerParams(vmem_limit_bytes=8 * MIB),
        cost_estimate=pl.CostEstimate(
            flops=2 * nodes * hidden * (nodes + cols),
            bytes_accessed=2 * nodes * nodes + 6 * cols * hidden,
            transcendentals=0,
        ),
    )(x_t, adj, col, *slopes)


def finish_kernel(n_dom, got_ref, sent_ref, *rest):
    at = lax.axis_index("dom")
    received = jnp.where((at == 0) | (at == n_dom - 1), 1.0, 0.0)
    got, sent = got_ref[...].astype(F32), sent_ref[...].astype(F32)
    rest[-1][0] = jnp.where(jnp.full(got.shape, received) > 0.5, got, sent)


def finish(place, shape, n_dom, got, sent, out):
    rows, cols = got.shape
    block = pl.BlockSpec((rows, cols), lambda i: (0, 0))
    before = [] if out is None else [out]
    return pl.pallas_call(
        functools.partial(finish_kernel, n_dom),
        name="finish",
        grid=(1,),
        out_shape=jax.ShapeDtypeStruct(shape, F32),
        in_specs=[block, block] + [pl.BlockSpec(memory_space=pl.ANY)] * len(before),
        out_specs=pl.BlockSpec((1, rows, cols), lambda i: (*place, 0)),
        input_output_aliases={2: 0} if before else {},
        compiler_params=pltpu.CompilerParams(vmem_limit_bytes=8 * MIB),
        cost_estimate=pl.CostEstimate(
            flops=2000000000, bytes_accessed=8 * rows * cols, transcendentals=0
        ),
    )(got, sent, *before)


def rounded(x):
    return lax.reduce_precision(x, 8, 7)


def chain_sum(chunks, n_dom, shape):
    half = n_dom // 2
    at = lax.axis_index("dom")
    inner = []
    for _, sent in chunks:
        for hop in range(half - 1):
            perm = [(hop, hop + 1), (n_dom - 1 - hop, n_dom - 2 - hop)]
            got = lax.ppermute(sent, "dom", perm)
            sent = rounded(sent.astype(F32) + got.astype(F32)).astype(BF16)
        inner.append(sent)
    middle = []
    for i, sent in enumerate(inner):
        if i >= 2:
            sent, _ = lax.optimization_barrier((sent, middle[i - 2]))
        got = lax.ppermute(sent, "dom", [(half - 1, half), (half, half - 1)])
        middle.append(rounded(sent.astype(F32) + got.astype(F32)).astype(BF16))
    out = None
    for i, sent in enumerate(middle):
        got = sent
        for hop in range(half - 1):
            low, high = half - 1 - hop, half + hop
            if hop:
                sent = jnp.where((at < low + 1) | (at > high - 1), got, sent)
            got = lax.ppermute(sent, "dom", [(low, low - 1), (high, high + 1)])
        out = finish(chunks[i][0], shape, n_dom, got, sent, out)
    return out


ORDER = (6, 4, 2, 0, 1, 3, 5, 7)


def swap(value, k, n_feat):
    return lax.ppermute(value, "feat", [(i, i ^ k) for i in range(n_feat)])


def reduce_pieces(pieces, n_feat):
    other = {k: swap(pieces[k + 1], 1, n_feat) for k in (6, 4, 2, 0)}
    terms = []
    for k in (6, 4, 2):
        chip = (pieces[k] + other[k].astype(F32)).astype(BF16)
        terms.append(swap(chip, k, n_feat))
    return terms + [other[0], pieces[0]]


def gather_pieces(piece, n_feat):
    got = {0: piece}
    for k in (6, 4, 2):
        got[k] = swap(piece, k, n_feat)
    for k in (0, 6, 4, 2):
        got[k + 1] = swap(got[k], 1, n_feat)
    return [got[k] for k in ORDER]


def dense_body(
    n_dom,
    n_feat,
    features,
    proj_weight,
    source_block,
    slot_count,
    block_pattern,
    node_type,
    type_gain,
    cotangent,
):
    source_block = jnp.transpose(source_block, (1, 2, 0))
    slot_count = jnp.transpose(slot_count, (1, 0))
    inv_deg, adj = adjacency(source_block, slot_count, block_pattern)
    pieces = forward(inv_deg, adj, features, proj_weight, n_feat)
    received = reduce_pieces(pieces, n_feat)
    x_t, col = transposed(features, inv_deg)
    received, x_t, col = lax.optimization_barrier((received, x_t, col))
    activations, slope = combine(received, node_type, type_gain, cotangent)
    slopes = gather_pieces(slope, n_feat)
    chunks = []
    for relation in range(proj_weight.shape[0]):
        parts = 2 if relation == 0 else 1
        made = gradient(parts, x_t, adj[relation], col[relation], slopes)
        chunks += [((relation, i), chunk) for i, chunk in enumerate(made)]
    shape = (proj_weight.shape[0], features.shape[1], proj_weight.shape[2])
    return activations, chain_sum(chunks, n_dom, shape)


def body(n_dom, n_feat, *args):
    nodes, relations = args[0].shape[0], args[2].shape[1]
    fits = 2 * relations * nodes * nodes <= 8 * MIB
    if fits and n_feat == 8 and n_dom % 2 == 0 and nodes == n_feat * BLK:
        return dense_body(n_dom, n_feat, *args)
    return general_body(*args)


def solution(mesh):
    placed = (
        P("dom", "feat"),
        P(None, "feat", None),
        P("dom", None, None),
        P("dom", None),
        P("dom", None, None, None, None),
        P(("dom", "feat")),
        P(),
        P(("dom", "feat"), None),
    )
    return jax.shard_map(
        functools.partial(body, mesh.shape["dom"], mesh.shape["feat"]),
        mesh=mesh,
        in_specs=placed,
        out_specs=(P(("dom", "feat"), None), P(None, "feat", None)),
        check_vma=False,
    )
```

```python
import functools

import jax
import jax.numpy as jnp
from jax import lax
from jax.experimental import pallas as pl
from jax.experimental.pallas import tpu as pltpu
from jax.sharding import PartitionSpec as P

BLK = 128
MIB = 1024 * 1024
BF16 = jnp.bfloat16
F32 = jnp.float32


def unpack_bits(packed):
    shifts = (2 ** jnp.arange(16)).astype(jnp.int32)
    bit_values = packed[..., None] // shifts % 2
    bit_values = jnp.swapaxes(bit_values, -3, -2)
    return bit_values.reshape(packed.shape[:-2] + (packed.shape[-1], packed.shape[-2] * 16))


def silu_grad(pre_act):
    sigmoid_value = jax.nn.sigmoid(pre_act)
    return sigmoid_value * (1.0 + pre_act * (1.0 - sigmoid_value))


def type_rows(node_type, type_gain):
    onehot = (
        node_type[:, None] == jnp.arange(type_gain.shape[0], dtype=jnp.int32)[None, :]
    ).astype(jnp.float32)
    return jnp.sum(onehot[:, :, None] * type_gain[None, :, :], axis=1)


def aggregate(features, source_block, slot_count, block_pattern):
    count_blocks = source_block.shape[0]
    relations = source_block.shape[1]
    slots_each = source_block.shape[2]
    col_width = features.shape[1]
    blocks = features.reshape(count_blocks, BLK, col_width)
    blocks_wide = blocks.astype(jnp.float32)
    live_slots = (
        jnp.arange(slots_each, dtype=jnp.int32)[None, None, :] < slot_count[:, :, None]
    ).astype(jnp.float32)
    mixed_list = []
    for relation in range(relations):
        summed = jnp.zeros((count_blocks, BLK, col_width), jnp.float32)
        degree = jnp.zeros((count_blocks, BLK), jnp.float32)
        for slot_index in range(slots_each):
            adjacency = (
                unpack_bits(block_pattern[:, relation, slot_index]).astype(jnp.float32)
                * live_slots[:, relation, slot_index][:, None, None]
            )
            picked = jnp.take(blocks, source_block[:, relation, slot_index], axis=0)
            summed = summed + jnp.einsum(
                "bij,bjc->bic",
                adjacency.astype(jnp.bfloat16),
                picked,
                preferred_element_type=jnp.float32,
            )
            degree = degree + jnp.sum(adjacency, axis=2)
        mixed_rows = ((blocks_wide + summed) / (1.0 + degree)[:, :, None]).astype(jnp.bfloat16)
        mixed_list.append(mixed_rows.reshape(count_blocks * BLK, col_width))
    return jnp.stack(mixed_list)


def general_body(
    features, proj_weight, source_block, slot_count, block_pattern, node_type, type_gain, cotangent
):
    mixed_all = aggregate(features, source_block, slot_count, block_pattern)
    pre_act = lax.psum_scatter(
        jnp.einsum("rnc,rch->nh", mixed_all, proj_weight, preferred_element_type=jnp.float32),
        "feat",
        scatter_dimension=0,
        tiled=True,
    )
    row_gains = type_rows(node_type, type_gain)
    output = (jax.nn.silu(pre_act) * row_gains).astype(jnp.bfloat16)
    slope_rows = (cotangent.astype(jnp.float32) * row_gains * silu_grad(pre_act)).astype(
        jnp.bfloat16
    )
    local_grad = jnp.einsum(
        "rnc,nh->rch",
        mixed_all,
        lax.all_gather(slope_rows, "feat", axis=0, tiled=True),
        preferred_element_type=jnp.float32,
    )
    weight_grad = lax.psum(local_grad, "dom")
    return (output, weight_grad)


def live_words(relation, slot, b, cnt_ref, pat_ref):
    live = jnp.where(slot < cnt_ref[relation, b], 0xFFFF, 0)
    return pat_ref[b, relation, slot] & live


def start_adjacency(places):
    sub = lax.broadcasted_iota(jnp.int32, (BLK, BLK), 0)
    lane = lax.broadcasted_iota(jnp.int32, (BLK, BLK), 1)
    eye = jnp.where(sub == lane, 1.0, 0.0).astype(BF16)
    for b, (ref, lanes) in enumerate(places):
        ref[:, lanes] = jnp.zeros((ref.shape[0], BLK), BF16)
        ref[b * BLK : (b + 1) * BLK, lanes] = eye


def add_edges(relation, places, src_ref, cnt_ref, pat_ref):
    bit = jnp.left_shift(1, lax.broadcasted_iota(jnp.int32, (16, BLK), 0))
    for s in range(src_ref.shape[1]):
        for b, (ref, lanes) in enumerate(places):
            words = live_words(relation, s, b, cnt_ref, pat_ref)
            row0 = pl.multiple_of(src_ref[relation, s, b] * BLK, BLK)
            parts = [
                jnp.where((words[w : w + 1, :] & bit) != 0, 1.0, 0.0)
                for w in range(words.shape[0])
            ]
            ref[pl.ds(row0, BLK), lanes] += jnp.concatenate(parts, axis=0).astype(BF16)


def inverse_degrees(relation, inv_ref, src_ref, cnt_ref, pat_ref):
    for b in range(src_ref.shape[2]):
        degree = jnp.zeros((8, BLK), jnp.int32)
        for s in range(src_ref.shape[1]):
            words = live_words(relation, s, b, cnt_ref, pat_ref)
            c = words - ((words >> 1) & 0x5555)
            c = (c & 0x3333) + ((c >> 2) & 0x3333)
            c = (c + (c >> 4)) & 0x0F0F
            degree = degree + ((c + (c >> 8)) & 0x1F)
        total = jnp.sum(degree.astype(F32), axis=0, keepdims=True)
        inv_ref[relation, 0:1, b * BLK : (b + 1) * BLK] = 1.0 / (1.0 + total)


def adjacency_kernel(src_ref, cnt_ref, pat_ref, inv_ref, *adj_refs):
    blocks = src_ref.shape[2]
    for relation, adj_ref in enumerate(adj_refs):
        places = [(adj_ref, slice(b * BLK, (b + 1) * BLK)) for b in range(blocks)]
        start_adjacency(places)
        inverse_degrees(relation, inv_ref, src_ref, cnt_ref, pat_ref)
        add_edges(relation, places, src_ref, cnt_ref, pat_ref)


def adjacency(source_block, slot_count, block_pattern):
    relations, _, blocks = source_block.shape
    nodes = blocks * BLK
    smem = pl.BlockSpec(memory_space=pltpu.SMEM)
    vmem = pl.BlockSpec(memory_space=pltpu.VMEM)
    inv_deg, *adj = pl.pallas_call(
        adjacency_kernel,
        name="adjacency",
        out_shape=[jax.ShapeDtypeStruct((relations, 8, nodes), F32)]
        + [jax.ShapeDtypeStruct((nodes, nodes), BF16)] * relations,
        in_specs=[smem, smem, vmem],
        out_specs=[vmem] * (1 + relations),
        compiler_params=pltpu.CompilerParams(vmem_limit_bytes=16 * MIB),
        cost_estimate=pl.CostEstimate(
            flops=1000 * relations * nodes * nodes,
            bytes_accessed=2 * relations * nodes * nodes,
            transcendentals=0,
        ),
    )(source_block, slot_count, block_pattern)
    return inv_deg, adj


def forward_kernel(n_feat, relations, inv_ref, *refs):
    adj_refs, refs = refs[:relations], refs[relations:]
    x_ref, w_ref, piece_refs, pre_ref = refs[0], refs[1], refs[2:-1], refs[-1]
    for relation in range(relations):
        y_t = lax.dot_general(
            w_ref[relation].T, x_ref[...], (((1,), (1,)), ((), ())), preferred_element_type=F32
        ).astype(BF16)
        p_t = jnp.dot(y_t, adj_refs[relation][...], preferred_element_type=F32)
        p_t = p_t * inv_ref[relation, 0:1, :]
        if relation == 0:
            pre_ref[...] = p_t
        else:
            pre_ref[...] += p_t

    me = lax.axis_index("feat")
    for k, piece in enumerate(piece_refs):
        first = pl.multiple_of((me ^ k) * BLK, BLK)
        piece[...] = pre_ref[:, pl.ds(first, BLK)].T.astype(piece.dtype)


def forward(inv_deg, adj, features, proj_weight, n_feat):
    nodes, cols = features.shape
    relations, _, hidden = proj_weight.shape
    vmem = pl.BlockSpec(memory_space=pltpu.VMEM)
    return pl.pallas_call(
        functools.partial(forward_kernel, n_feat, relations),
        name="forward",
        out_shape=[
            jax.ShapeDtypeStruct((nodes // n_feat, hidden), BF16 if k % 2 else F32)
            for k in range(n_feat)
        ],
        in_specs=[vmem] * (3 + relations),
        out_specs=[vmem] * n_feat,
        scratch_shapes=[pltpu.VMEM((hidden, nodes), F32)],
        compiler_params=pltpu.CompilerParams(vmem_limit_bytes=16 * MIB),
        cost_estimate=pl.CostEstimate(
            flops=2 * relations * nodes * hidden * (nodes + cols),
            bytes_accessed=2 * relations * nodes * nodes,
            transcendentals=0,
        ),
    )(inv_deg, *adj, features, proj_weight)


def transposed_kernel(x_ref, inv_ref, xt_ref, *col_refs):
    nodes = x_ref.shape[0]
    for b in range(nodes // BLK):
        rows = slice(b * BLK, (b + 1) * BLK)
        xt_ref[:, rows] = x_ref[rows, :].T
        for r, col_ref in enumerate(col_refs):
            wide = jnp.broadcast_to(inv_ref[r, 0:1, rows], (BLK, BLK))
            col_ref[rows, :] = wide.T


def transposed(features, inv_deg):
    nodes, cols = features.shape
    relations = inv_deg.shape[0]
    x_t, *col = pl.pallas_call(
        transposed_kernel,
        name="transposed",
        out_shape=[jax.ShapeDtypeStruct((cols, nodes), BF16)]
        + [jax.ShapeDtypeStruct((nodes, BLK), F32)] * relations,
        compiler_params=pltpu.CompilerParams(vmem_limit_bytes=8 * MIB),
        cost_estimate=pl.CostEstimate(
            flops=2 * nodes * cols, bytes_accessed=6 * nodes * cols, transcendentals=0
        ),
    )(features, inv_deg)
    return x_t, col


def combine_kernel(n_feat, *refs):
    type_ref, gain_ref, cot_ref, act_ref, slope_ref = refs[n_feat:]
    rows = act_ref.shape[0]
    pre = refs[0][...].astype(F32)
    for piece in refs[1:n_feat]:
        pre = pre + piece[...].astype(F32)
    types = jnp.broadcast_to(type_ref[...].astype(F32), (rows, rows)).T
    types = jnp.concatenate([types] * (act_ref.shape[1] // rows), axis=1)
    gain = jnp.zeros(act_ref.shape, F32)
    for t in range(gain_ref.shape[0]):
        gain = jnp.where(types == t, gain_ref[t : t + 1, :], gain)
    sig = jax.nn.sigmoid(pre)
    act_ref[...] = (pre * sig * gain).astype(BF16)
    grad = sig * (1.0 + pre * (1.0 - sig))
    slope_ref[...] = (cot_ref[...].astype(F32) * gain * grad).astype(BF16)


def combine(pieces, node_type, type_gain, cotangent):
    return pl.pallas_call(
        functools.partial(combine_kernel, len(pieces)),
        name="combine",
        out_shape=[jax.ShapeDtypeStruct(cotangent.shape, BF16)] * 2,
        compiler_params=pltpu.CompilerParams(vmem_limit_bytes=6 * MIB),
    )(*pieces, node_type[None, :], type_gain, cotangent)


def gradient_kernel(n_feat, xt_ref, adj_ref, col_ref, *rest):
    sent_refs, scaled_ref = rest[n_feat:-1], rest[-1]
    me = lax.axis_index("feat")
    for k, piece in zip(ORDER, rest[:n_feat]):
        rows = pl.ds(pl.multiple_of((me ^ k) * BLK, BLK), BLK)
        inv = jnp.concatenate([col_ref[rows, :]] * (piece.shape[1] // BLK), axis=1)
        scaled_ref[rows, :] = (piece[...].astype(F32) * inv).astype(BF16)
    spread = jnp.dot(adj_ref[...], scaled_ref[...], preferred_element_type=F32).astype(BF16)
    rows = xt_ref.shape[0] // len(sent_refs)
    for i, sent_ref in enumerate(sent_refs):
        x_t = xt_ref[i * rows : (i + 1) * rows, :]
        sent_ref[...] = jnp.dot(x_t, spread, preferred_element_type=F32).astype(BF16)


def gradient(parts, x_t, adj, col, slopes):
    cols, nodes = x_t.shape
    hidden = slopes[0].shape[1]
    vmem = pl.BlockSpec(memory_space=pltpu.VMEM)
    return pl.pallas_call(
        functools.partial(gradient_kernel, len(slopes)),
        name="gradient",
        out_shape=[jax.ShapeDtypeStruct((cols // parts, hidden), BF16)] * parts,
        in_specs=[vmem] * (3 + len(slopes)),
        out_specs=[vmem] * parts,
        scratch_shapes=[pltpu.VMEM((nodes, hidden), BF16)],
        compiler_params=pltpu.CompilerParams(vmem_limit_bytes=8 * MIB),
        cost_estimate=pl.CostEstimate(
            flops=2 * nodes * hidden * (nodes + cols),
            bytes_accessed=2 * nodes * nodes + 6 * cols * hidden,
            transcendentals=0,
        ),
    )(x_t, adj, col, *slopes)


def finish_kernel(n_dom, got_ref, sent_ref, *rest):
    at = lax.axis_index("dom")
    received = jnp.where((at == 0) | (at == n_dom - 1), 1.0, 0.0)
    got, sent = got_ref[...].astype(F32), sent_ref[...].astype(F32)
    rest[-1][0] = jnp.where(jnp.full(got.shape, received) > 0.5, got, sent)


def finish(place, shape, n_dom, got, sent, out):
    rows, cols = got.shape
    block = pl.BlockSpec((rows, cols), lambda i: (0, 0))
    before = [] if out is None else [out]
    return pl.pallas_call(
        functools.partial(finish_kernel, n_dom),
        name="finish",
        grid=(1,),
        out_shape=jax.ShapeDtypeStruct(shape, F32),
        in_specs=[block, block] + [pl.BlockSpec(memory_space=pl.ANY)] * len(before),
        out_specs=pl.BlockSpec((1, rows, cols), lambda i: (*place, 0)),
        input_output_aliases={2: 0} if before else {},
        compiler_params=pltpu.CompilerParams(vmem_limit_bytes=8 * MIB),
        cost_estimate=pl.CostEstimate(
            flops=2000000000, bytes_accessed=8 * rows * cols, transcendentals=0
        ),
    )(got, sent, *before)


def rounded(x):
    return lax.reduce_precision(x, 8, 7)


def chain_sum(chunks, n_dom, shape):
    half = n_dom // 2
    at = lax.axis_index("dom")
    inner = []
    for _, sent in chunks:
        for hop in range(half - 1):
            perm = [(hop, hop + 1), (n_dom - 1 - hop, n_dom - 2 - hop)]
            got = lax.ppermute(sent, "dom", perm)
            sent = rounded(sent.astype(F32) + got.astype(F32)).astype(BF16)
        inner.append(sent)
    middle = []
    for i, sent in enumerate(inner):
        if i >= 2:
            sent, _ = lax.optimization_barrier((sent, middle[i - 2]))
        got = lax.ppermute(sent, "dom", [(half - 1, half), (half, half - 1)])
        middle.append(rounded(sent.astype(F32) + got.astype(F32)).astype(BF16))
    out = None
    for i, sent in enumerate(middle):
        got = sent
        for hop in range(half - 1):
            low, high = half - 1 - hop, half + hop
            if hop:
                sent = jnp.where((at < low + 1) | (at > high - 1), got, sent)
            got = lax.ppermute(sent, "dom", [(low, low - 1), (high, high + 1)])
        out = finish(chunks[i][0], shape, n_dom, got, sent, out)
    return out


ORDER = (6, 4, 2, 0, 1, 3, 5, 7)


def swap(value, k, n_feat):
    return lax.ppermute(value, "feat", [(i, i ^ k) for i in range(n_feat)])


def reduce_pieces(pieces, n_feat):
    other = {k: swap(pieces[k + 1], 1, n_feat) for k in (6, 4, 2, 0)}
    terms = []
    for k in (6, 4, 2):
        chip = (pieces[k] + other[k].astype(F32)).astype(BF16)
        terms.append(swap(chip, k, n_feat))
    return terms + [other[0], pieces[0]]


def gather_pieces(piece, n_feat):
    got = {0: piece}
    for k in (6, 4, 2):
        got[k] = swap(piece, k, n_feat)
    for k in (0, 6, 4, 2):
        got[k + 1] = swap(got[k], 1, n_feat)
    return [got[k] for k in ORDER]


def dense_body(
    n_dom,
    n_feat,
    features,
    proj_weight,
    source_block,
    slot_count,
    block_pattern,
    node_type,
    type_gain,
    cotangent,
):
    source_block = jnp.transpose(source_block, (1, 2, 0))
    slot_count = jnp.transpose(slot_count, (1, 0))
    inv_deg, adj = adjacency(source_block, slot_count, block_pattern)
    pieces = forward(inv_deg, adj, features, proj_weight, n_feat)
    received = reduce_pieces(pieces, n_feat)
    x_t, col = transposed(features, inv_deg)
    activations, slope = combine(received, node_type, type_gain, cotangent)
    slopes = gather_pieces(slope, n_feat)
    chunks = []
    for relation in range(proj_weight.shape[0]):
        parts = 2 if relation == 0 else 1
        made = gradient(parts, x_t, adj[relation], col[relation], slopes)
        x_t, *made = lax.optimization_barrier((x_t, *made))
        chunks += [((relation, i), chunk) for i, chunk in enumerate(made)]
    chunks = chunks[:2] + chunks[:1:-1]
    shape = (proj_weight.shape[0], features.shape[1], proj_weight.shape[2])
    return activations, chain_sum(chunks, n_dom, shape)


def body(n_dom, n_feat, *args):
    nodes, relations = args[0].shape[0], args[2].shape[1]
    fits = 2 * relations * nodes * nodes <= 8 * MIB
    if fits and n_feat == 8 and n_dom % 2 == 0 and nodes == n_feat * BLK:
        return dense_body(n_dom, n_feat, *args)
    return general_body(*args)


def solution(mesh):
    placed = (
        P("dom", "feat"),
        P(None, "feat", None),
        P("dom", None, None),
        P("dom", None),
        P("dom", None, None, None, None),
        P(("dom", "feat")),
        P(),
        P(("dom", "feat"), None),
    )
    return jax.shard_map(
        functools.partial(body, mesh.shape["dom"], mesh.shape["feat"]),
        mesh=mesh,
        in_specs=placed,
        out_specs=(P(("dom", "feat"), None), P(None, "feat", None)),
        check_vma=False,
    )
```

```python
import functools

import jax
import jax.numpy as jnp
from jax import lax
from jax.experimental import pallas as pl
from jax.experimental.pallas import tpu as pltpu
from jax.sharding import PartitionSpec as P

BLK = 128
MIB = 1024 * 1024
BF16 = jnp.bfloat16
F32 = jnp.float32


def unpack_bits(packed):
    shifts = (2 ** jnp.arange(16)).astype(jnp.int32)
    bit_values = packed[..., None] // shifts % 2
    bit_values = jnp.swapaxes(bit_values, -3, -2)
    return bit_values.reshape(packed.shape[:-2] + (packed.shape[-1], packed.shape[-2] * 16))


def silu_grad(pre_act):
    sigmoid_value = jax.nn.sigmoid(pre_act)
    return sigmoid_value * (1.0 + pre_act * (1.0 - sigmoid_value))


def type_rows(node_type, type_gain):
    onehot = (
        node_type[:, None] == jnp.arange(type_gain.shape[0], dtype=jnp.int32)[None, :]
    ).astype(jnp.float32)
    return jnp.sum(onehot[:, :, None] * type_gain[None, :, :], axis=1)


def aggregate(features, source_block, slot_count, block_pattern):
    count_blocks = source_block.shape[0]
    relations = source_block.shape[1]
    slots_each = source_block.shape[2]
    col_width = features.shape[1]
    blocks = features.reshape(count_blocks, BLK, col_width)
    blocks_wide = blocks.astype(jnp.float32)
    live_slots = (
        jnp.arange(slots_each, dtype=jnp.int32)[None, None, :] < slot_count[:, :, None]
    ).astype(jnp.float32)
    mixed_list = []
    for relation in range(relations):
        summed = jnp.zeros((count_blocks, BLK, col_width), jnp.float32)
        degree = jnp.zeros((count_blocks, BLK), jnp.float32)
        for slot_index in range(slots_each):
            adjacency = (
                unpack_bits(block_pattern[:, relation, slot_index]).astype(jnp.float32)
                * live_slots[:, relation, slot_index][:, None, None]
            )
            picked = jnp.take(blocks, source_block[:, relation, slot_index], axis=0)
            summed = summed + jnp.einsum(
                "bij,bjc->bic",
                adjacency.astype(jnp.bfloat16),
                picked,
                preferred_element_type=jnp.float32,
            )
            degree = degree + jnp.sum(adjacency, axis=2)
        mixed_rows = ((blocks_wide + summed) / (1.0 + degree)[:, :, None]).astype(jnp.bfloat16)
        mixed_list.append(mixed_rows.reshape(count_blocks * BLK, col_width))
    return jnp.stack(mixed_list)


def general_body(
    features, proj_weight, source_block, slot_count, block_pattern, node_type, type_gain, cotangent
):
    mixed_all = aggregate(features, source_block, slot_count, block_pattern)
    pre_act = lax.psum_scatter(
        jnp.einsum("rnc,rch->nh", mixed_all, proj_weight, preferred_element_type=jnp.float32),
        "feat",
        scatter_dimension=0,
        tiled=True,
    )
    row_gains = type_rows(node_type, type_gain)
    output = (jax.nn.silu(pre_act) * row_gains).astype(jnp.bfloat16)
    slope_rows = (cotangent.astype(jnp.float32) * row_gains * silu_grad(pre_act)).astype(
        jnp.bfloat16
    )
    local_grad = jnp.einsum(
        "rnc,nh->rch",
        mixed_all,
        lax.all_gather(slope_rows, "feat", axis=0, tiled=True),
        preferred_element_type=jnp.float32,
    )
    weight_grad = lax.psum(local_grad, "dom")
    return (output, weight_grad)


def live_words(relation, slot, b, cnt_ref, pat_ref):
    live = jnp.where(slot < cnt_ref[relation, b], 0xFFFF, 0)
    return pat_ref[b, relation, slot] & live


def start_adjacency(places):
    sub = lax.broadcasted_iota(jnp.int32, (BLK, BLK), 0)
    lane = lax.broadcasted_iota(jnp.int32, (BLK, BLK), 1)
    eye = jnp.where(sub == lane, 1.0, 0.0).astype(BF16)
    for b, (ref, lanes) in enumerate(places):
        ref[:, lanes] = jnp.zeros((ref.shape[0], BLK), BF16)
        ref[b * BLK : (b + 1) * BLK, lanes] = eye


def add_edges(relation, places, src_ref, cnt_ref, pat_ref):
    bit = jnp.left_shift(1, lax.broadcasted_iota(jnp.int32, (16, BLK), 0))
    for s in range(src_ref.shape[1]):
        for b, (ref, lanes) in enumerate(places):
            words = live_words(relation, s, b, cnt_ref, pat_ref)
            row0 = pl.multiple_of(src_ref[relation, s, b] * BLK, BLK)
            parts = [
                jnp.where((words[w : w + 1, :] & bit) != 0, 1.0, 0.0)
                for w in range(words.shape[0])
            ]
            ref[pl.ds(row0, BLK), lanes] += jnp.concatenate(parts, axis=0).astype(BF16)


def inverse_degrees(relation, inv_ref, src_ref, cnt_ref, pat_ref):
    for b in range(src_ref.shape[2]):
        degree = jnp.zeros((8, BLK), jnp.int32)
        for s in range(src_ref.shape[1]):
            words = live_words(relation, s, b, cnt_ref, pat_ref)
            c = words - ((words >> 1) & 0x5555)
            c = (c & 0x3333) + ((c >> 2) & 0x3333)
            c = (c + (c >> 4)) & 0x0F0F
            degree = degree + ((c + (c >> 8)) & 0x1F)
        total = jnp.sum(degree.astype(F32), axis=0, keepdims=True)
        inv_ref[relation, 0:1, b * BLK : (b + 1) * BLK] = 1.0 / (1.0 + total)


def adjacency_kernel(src_ref, cnt_ref, pat_ref, inv_ref, *adj_refs):
    blocks = src_ref.shape[2]
    for relation, adj_ref in enumerate(adj_refs):
        places = [(adj_ref, slice(b * BLK, (b + 1) * BLK)) for b in range(blocks)]
        start_adjacency(places)
        inverse_degrees(relation, inv_ref, src_ref, cnt_ref, pat_ref)
        add_edges(relation, places, src_ref, cnt_ref, pat_ref)


def adjacency(source_block, slot_count, block_pattern):
    relations, _, blocks = source_block.shape
    nodes = blocks * BLK
    smem = pl.BlockSpec(memory_space=pltpu.SMEM)
    vmem = pl.BlockSpec(memory_space=pltpu.VMEM)
    inv_deg, *adj = pl.pallas_call(
        adjacency_kernel,
        name="adjacency",
        out_shape=[jax.ShapeDtypeStruct((relations, 8, nodes), F32)]
        + [jax.ShapeDtypeStruct((nodes, nodes), BF16)] * relations,
        in_specs=[smem, smem, vmem],
        out_specs=[vmem] * (1 + relations),
        compiler_params=pltpu.CompilerParams(vmem_limit_bytes=16 * MIB),
        cost_estimate=pl.CostEstimate(
            flops=1000 * relations * nodes * nodes,
            bytes_accessed=2 * relations * nodes * nodes,
            transcendentals=0,
        ),
    )(source_block, slot_count, block_pattern)
    return inv_deg, adj


def forward_kernel(n_feat, relations, inv_ref, *refs):
    adj_refs, refs = refs[:relations], refs[relations:]
    x_ref, w_ref, piece_refs, pre_ref = refs[0], refs[1], refs[2:-1], refs[-1]
    for relation in range(relations):
        y_t = lax.dot_general(
            w_ref[relation].T, x_ref[...], (((1,), (1,)), ((), ())), preferred_element_type=F32
        ).astype(BF16)
        p_t = jnp.dot(y_t, adj_refs[relation][...], preferred_element_type=F32)
        p_t = p_t * inv_ref[relation, 0:1, :]
        if relation == 0:
            pre_ref[...] = p_t
        else:
            pre_ref[...] += p_t

    me = lax.axis_index("feat")
    for k, piece in enumerate(piece_refs):
        first = pl.multiple_of((me ^ k) * BLK, BLK)
        piece[...] = pre_ref[:, pl.ds(first, BLK)].T.astype(piece.dtype)


def forward(inv_deg, adj, features, proj_weight, n_feat):
    nodes, cols = features.shape
    relations, _, hidden = proj_weight.shape
    vmem = pl.BlockSpec(memory_space=pltpu.VMEM)
    return pl.pallas_call(
        functools.partial(forward_kernel, n_feat, relations),
        name="forward",
        out_shape=[
            jax.ShapeDtypeStruct((nodes // n_feat, hidden), BF16 if k % 2 else F32)
            for k in range(n_feat)
        ],
        in_specs=[vmem] * (3 + relations),
        out_specs=[vmem] * n_feat,
        scratch_shapes=[pltpu.VMEM((hidden, nodes), F32)],
        compiler_params=pltpu.CompilerParams(vmem_limit_bytes=16 * MIB),
        cost_estimate=pl.CostEstimate(
            flops=2 * relations * nodes * hidden * (nodes + cols),
            bytes_accessed=2 * relations * nodes * nodes,
            transcendentals=0,
        ),
    )(inv_deg, *adj, features, proj_weight)


def transposed_kernel(x_ref, inv_ref, xt_ref, *col_refs):
    nodes = x_ref.shape[0]
    for b in range(nodes // BLK):
        rows = slice(b * BLK, (b + 1) * BLK)
        xt_ref[:, rows] = x_ref[rows, :].T
        for r, col_ref in enumerate(col_refs):
            wide = jnp.broadcast_to(inv_ref[r, 0:1, rows], (BLK, BLK))
            col_ref[rows, :] = wide.T


def transposed(features, inv_deg):
    nodes, cols = features.shape
    relations = inv_deg.shape[0]
    x_t, *col = pl.pallas_call(
        transposed_kernel,
        name="transposed",
        out_shape=[jax.ShapeDtypeStruct((cols, nodes), BF16)]
        + [jax.ShapeDtypeStruct((nodes, BLK), F32)] * relations,
        compiler_params=pltpu.CompilerParams(vmem_limit_bytes=8 * MIB),
        cost_estimate=pl.CostEstimate(
            flops=2 * nodes * cols, bytes_accessed=6 * nodes * cols, transcendentals=0
        ),
    )(features, inv_deg)
    return x_t, col


def combine_kernel(n_feat, *refs):
    type_ref, gain_ref, cot_ref, act_ref, slope_ref = refs[n_feat:]
    rows = act_ref.shape[0]
    pre = refs[0][...].astype(F32)
    for piece in refs[1:n_feat]:
        pre = pre + piece[...].astype(F32)
    types = jnp.broadcast_to(type_ref[...].astype(F32), (rows, rows)).T
    types = jnp.concatenate([types] * (act_ref.shape[1] // rows), axis=1)
    gain = jnp.zeros(act_ref.shape, F32)
    for t in range(gain_ref.shape[0]):
        gain = jnp.where(types == t, gain_ref[t : t + 1, :], gain)
    sig = jax.nn.sigmoid(pre)
    act_ref[...] = (pre * sig * gain).astype(BF16)
    grad = sig * (1.0 + pre * (1.0 - sig))
    slope_ref[...] = (cot_ref[...].astype(F32) * gain * grad).astype(BF16)


def combine(pieces, node_type, type_gain, cotangent):
    return pl.pallas_call(
        functools.partial(combine_kernel, len(pieces)),
        name="combine",
        out_shape=[jax.ShapeDtypeStruct(cotangent.shape, BF16)] * 2,
        compiler_params=pltpu.CompilerParams(vmem_limit_bytes=6 * MIB),
    )(*pieces, node_type[None, :], type_gain, cotangent)


def gradient_kernel(n_feat, xt_ref, adj_ref, col_ref, *rest):
    sent_refs, scaled_ref = rest[n_feat:-1], rest[-1]
    me = lax.axis_index("feat")
    for k, piece in zip(ORDER, rest[:n_feat]):
        rows = pl.ds(pl.multiple_of((me ^ k) * BLK, BLK), BLK)
        inv = jnp.concatenate([col_ref[rows, :]] * (piece.shape[1] // BLK), axis=1)
        scaled_ref[rows, :] = (piece[...].astype(F32) * inv).astype(BF16)
    spread = jnp.dot(adj_ref[...], scaled_ref[...], preferred_element_type=F32).astype(BF16)
    rows = xt_ref.shape[0] // len(sent_refs)
    for i, sent_ref in enumerate(sent_refs):
        x_t = xt_ref[i * rows : (i + 1) * rows, :]
        sent_ref[...] = jnp.dot(x_t, spread, preferred_element_type=F32).astype(BF16)


def gradient(parts, x_t, adj, col, slopes):
    cols, nodes = x_t.shape
    hidden = slopes[0].shape[1]
    vmem = pl.BlockSpec(memory_space=pltpu.VMEM)
    return pl.pallas_call(
        functools.partial(gradient_kernel, len(slopes)),
        name="gradient",
        out_shape=[jax.ShapeDtypeStruct((cols // parts, hidden), BF16)] * parts,
        in_specs=[vmem] * (3 + len(slopes)),
        out_specs=[vmem] * parts,
        scratch_shapes=[pltpu.VMEM((nodes, hidden), BF16)],
        compiler_params=pltpu.CompilerParams(vmem_limit_bytes=8 * MIB),
        cost_estimate=pl.CostEstimate(
            flops=2 * nodes * hidden * (nodes + cols),
            bytes_accessed=2 * nodes * nodes + 6 * cols * hidden,
            transcendentals=0,
        ),
    )(x_t, adj, col, *slopes)


def finish_kernel(n_dom, got_ref, sent_ref, *rest):
    at = lax.axis_index("dom")
    received = jnp.where((at == 0) | (at == n_dom - 1), 1.0, 0.0)
    got, sent = got_ref[...].astype(F32), sent_ref[...].astype(F32)
    rest[-1][0] = jnp.where(jnp.full(got.shape, received) > 0.5, got, sent)


def finish(place, shape, n_dom, got, sent, out):
    rows, cols = got.shape
    block = pl.BlockSpec((rows, cols), lambda i: (0, 0))
    before = [] if out is None else [out]
    return pl.pallas_call(
        functools.partial(finish_kernel, n_dom),
        name="finish",
        grid=(1,),
        out_shape=jax.ShapeDtypeStruct(shape, F32),
        in_specs=[block, block] + [pl.BlockSpec(memory_space=pl.ANY)] * len(before),
        out_specs=pl.BlockSpec((1, rows, cols), lambda i: (*place, 0)),
        input_output_aliases={2: 0} if before else {},
        compiler_params=pltpu.CompilerParams(vmem_limit_bytes=8 * MIB),
        cost_estimate=pl.CostEstimate(
            flops=2000000000, bytes_accessed=8 * rows * cols, transcendentals=0
        ),
    )(got, sent, *before)


def rounded(x):
    return lax.reduce_precision(x, 8, 7)


def chain_sum(chunks, n_dom, shape):
    half = n_dom // 2
    at = lax.axis_index("dom")
    inner = []
    for _, sent in chunks:
        for hop in range(half - 1):
            perm = [(hop, hop + 1), (n_dom - 1 - hop, n_dom - 2 - hop)]
            got = lax.ppermute(sent, "dom", perm)
            sent = rounded(sent.astype(F32) + got.astype(F32)).astype(BF16)
        inner.append(sent)
    middle = []
    for i, sent in enumerate(inner):
        if i == 3:
            sent, _ = lax.optimization_barrier((sent, middle[i - 2]))
        got = lax.ppermute(sent, "dom", [(half - 1, half), (half, half - 1)])
        if i == 1 and len(inner) > 2:
            got, _ = lax.optimization_barrier((got, inner[2]))
        middle.append(rounded(sent.astype(F32) + got.astype(F32)).astype(BF16))
    out = None
    for i, sent in enumerate(middle):
        got = sent
        for hop in range(half - 1):
            low, high = half - 1 - hop, half + hop
            if hop:
                sent = jnp.where((at < low + 1) | (at > high - 1), got, sent)
            got = lax.ppermute(sent, "dom", [(low, low - 1), (high, high + 1)])
        out = finish(chunks[i][0], shape, n_dom, got, sent, out)
    return out


ORDER = (6, 4, 2, 0, 1, 3, 5, 7)


def swap(value, k, n_feat):
    return lax.ppermute(value, "feat", [(i, i ^ k) for i in range(n_feat)])


def reduce_pieces(pieces, n_feat):
    other = {k: swap(pieces[k + 1], 1, n_feat) for k in (6, 4, 2, 0)}
    terms = []
    for k in (6, 4, 2):
        chip = (pieces[k] + other[k].astype(F32)).astype(BF16)
        terms.append(swap(chip, k, n_feat))
    return terms + [other[0], pieces[0]]


def gather_pieces(piece, n_feat):
    got = {0: piece}
    for k in (6, 4, 2):
        got[k] = swap(piece, k, n_feat)
    for k in (0, 6, 4, 2):
        got[k + 1] = swap(got[k], 1, n_feat)
    return [got[k] for k in ORDER]


def dense_body(
    n_dom,
    n_feat,
    features,
    proj_weight,
    source_block,
    slot_count,
    block_pattern,
    node_type,
    type_gain,
    cotangent,
):
    source_block = jnp.transpose(source_block, (1, 2, 0))
    slot_count = jnp.transpose(slot_count, (1, 0))
    inv_deg, adj = adjacency(source_block, slot_count, block_pattern)
    pieces = forward(inv_deg, adj, features, proj_weight, n_feat)
    received = reduce_pieces(pieces, n_feat)
    x_t, col = transposed(features, inv_deg)
    activations, slope = combine(received, node_type, type_gain, cotangent)
    slopes = gather_pieces(slope, n_feat)
    chunks = []
    for relation in range(proj_weight.shape[0]):
        parts = 2 if relation == 0 else 1
        made = gradient(parts, x_t, adj[relation], col[relation], slopes)
        x_t, *made = lax.optimization_barrier((x_t, *made))
        chunks += [((relation, i), chunk) for i, chunk in enumerate(made)]
    chunks = chunks[:2] + chunks[:1:-1]
    shape = (proj_weight.shape[0], features.shape[1], proj_weight.shape[2])
    return activations, chain_sum(chunks, n_dom, shape)


def body(n_dom, n_feat, *args):
    nodes, relations = args[0].shape[0], args[2].shape[1]
    fits = 2 * relations * nodes * nodes <= 8 * MIB
    if fits and n_feat == 8 and n_dom % 2 == 0 and nodes == n_feat * BLK:
        return dense_body(n_dom, n_feat, *args)
    return general_body(*args)


def solution(mesh):
    placed = (
        P("dom", "feat"),
        P(None, "feat", None),
        P("dom", None, None),
        P("dom", None),
        P("dom", None, None, None, None),
        P(("dom", "feat")),
        P(),
        P(("dom", "feat"), None),
    )
    return jax.shard_map(
        functools.partial(body, mesh.shape["dom"], mesh.shape["feat"]),
        mesh=mesh,
        in_specs=placed,
        out_specs=(P(("dom", "feat"), None), P(None, "feat", None)),
        check_vma=False,
    )
```
